128 devices in a mesh: grp: 8 (over y, core), exp: 16 (over x, z).
Axes of the slice: x: 4, y: 4, z: 4, core: 2. Of those that a mesh axis runs over, the one named last changes fastest.
Arguments:
- tokens: bfloat16 [1024, 7168], P(('grp', 'exp')), may hold values from -6 to 6
- routes: int32 [1024, 8], P(('grp', 'exp')), may hold values from 0 to 63, as said below
- weights_q: int32 [1024, 8], P(('grp', 'exp')), may hold values from 1 to 255
- cotangent: bfloat16 [1024, 7168], P(('grp', 'exp')), may hold values from -6 to 6
- expert_gate: bfloat16 [128, 7168, 512], P(('grp', 'exp')), may hold values from -0.0625 to 0.0625
- expert_up: bfloat16 [128, 7168, 512], P(('grp', 'exp')), may hold values from -0.0625 to 0.0625
- expert_down: bfloat16 [128, 512, 7168], P(('grp', 'exp')), may hold values from -0.1875 to 0.1875
- shared_gate: bfloat16 [7168, 1024], P(None, 'exp'), may hold values from -0.0625 to 0.0625
- shared_up: bfloat16 [7168, 1024], P(None, 'exp'), may hold values from -0.0625 to 0.0625
- shared_down: bfloat16 [1024, 7168], P('exp'), may hold values from -0.1875 to 0.1875
Outputs:
- mixed: bfloat16 [1024, 7168], P(('grp', 'exp'))
- token_grad: bfloat16 [1024, 7168], P(('grp', 'exp'))
The draws below stay inside these ranges and needn't reach their ends.
Inputs may be any that keep to these rules, and one draw needn't show every extreme that they name: `routes`: each row names 8 different experts, 2 of them in each of 4 different groups, where expert e belongs to group e // 8. Among the rows of one device (aligned blocks of 8 rows) no expert is named more than 2 times.
All inputs are finite; a program needn't handle non-finite values.
Results may differ from the reference program's by a relative error of at most 0.014.
Values may be sent and summed in bfloat16 or wider, within the bound.
No kernel may reach another device: no remote copies, remote signals or barrier semaphores. Data moves between devices by JAX's collectives and lax.ppermute only.
A program may use at most 128 MiB of HBM per device.

```python
import jax
import jax.numpy as jnp
from jax import lax

D = 7168
HID = 1024
SH_HID = 1024
SPLIT = 2
TOP = 8
GROUPS_TOK = 4
TOK_DEV = 8
GROUPS = 8
EXP_GRP = 8
EXPERTS = 64
HID_DEV = 512
CAP = 2
TOKENS = 1024
N_GRP = 8
N_EXP = 16


def draw_routes(key, part):
    key = jax.random.fold_in(key, 7)
    key_list = jax.random.split(key, 4)
    blocks = TOKENS // TOK_DEV
    per_group = TOP // GROUPS_TOK
    hot_group = jax.random.randint(key_list[0], (), 0, GROUPS)
    group_ids = jnp.arange(GROUPS, dtype=jnp.int32)
    group_noise = jax.random.randint(key_list[1], (blocks, TOK_DEV, GROUPS), 0, 1 << 20)
    group_score = jnp.where(group_ids == hot_group, -1, group_noise * GROUPS + group_ids)
    group_order = jnp.argsort(group_score, axis=-1)
    chosen = group_order[:, :, :GROUPS_TOK].astype(jnp.int32)
    touched = jnp.sum((chosen[:, :, :, None] == group_ids).astype(jnp.int32), axis=2)
    token_rank = jnp.cumsum(touched, axis=1) - touched
    rank_chosen = jnp.take_along_axis(token_rank, chosen, axis=2)
    expert_noise = jax.random.randint(key_list[2], (blocks, GROUPS, EXP_GRP), 0, 1 << 20)
    expert_perm = jnp.argsort(expert_noise * EXP_GRP + jnp.arange(EXP_GRP, dtype=jnp.int32), axis=-1).astype(jnp.int32)
    perm_tokens = jnp.broadcast_to(expert_perm[:, None], (blocks, TOK_DEV, GROUPS, EXP_GRP))
    group_index = jnp.broadcast_to(chosen[:, :, :, None], (blocks, TOK_DEV, GROUPS_TOK, EXP_GRP))
    perm_chosen = jnp.take_along_axis(perm_tokens, group_index, axis=2)
    positions = (rank_chosen[:, :, :, None] * per_group + jnp.arange(per_group, dtype=jnp.int32)) % EXP_GRP
    local_ids = jnp.take_along_axis(perm_chosen, positions, axis=3)
    expert_ids = (chosen[:, :, :, None] * EXP_GRP + local_ids).reshape(blocks, TOK_DEV, TOP)
    shuffle_noise = jax.random.randint(key_list[3], (blocks, TOK_DEV, TOP), 0, 1 << 20)
    shuffle = jnp.argsort(shuffle_noise * TOP + jnp.arange(TOP, dtype=jnp.int32), axis=-1)
    expert_ids = jnp.take_along_axis(expert_ids, shuffle, axis=2)
    return expert_ids.reshape(TOKENS, TOP).astype(jnp.int32)


def touch_ends(drawn, rng, low, largest):
    extent = drawn.shape
    index_at = [jax.random.randint(jax.random.fold_in(rng, axis), (), 0, extent[axis]) for axis in range(len(extent))]
    drawn = drawn.at[tuple(index_at)].set(low)
    longest = extent.index(max(extent))
    index_at[longest] = (index_at[longest] + 1) % extent[longest]
    return drawn.at[tuple(index_at)].set(largest)


def level_of(own_key, shape, shards, least, high):
    factor_of = 1.0
    for axis_at, blocks in shards:
        steps = jax.random.uniform(jax.random.fold_in(jax.random.fold_in(own_key, 6), axis_at), (blocks,), jnp.float32, least / len(shards), high / len(shards))
        factor_of = factor_of * jnp.repeat(jnp.exp(steps), shape[axis_at] // blocks).reshape((-1,) + (1,) * (len(shape) - 1 - axis_at))
    return factor_of


def scatter_about(rng, dims, spread, most, pieces=(), kind=jnp.bfloat16):
    values = jax.random.normal(rng, dims, jnp.float32) * spread
    if len(pieces) > 0:
        values = level_of(rng, dims, pieces, -0.22, 0.18) * values
    return jnp.clip(values, min=-most, max=most).astype(kind)


def setup_inputs(seed: int = 0) -> dict:
    streams_of = jax.random.split(jax.random.key(seed), 11)
    tokens = scatter_about(streams_of[0], (TOKENS, D), 1.0, 6.0, ((0, 128),))
    routes = draw_routes(jax.random.fold_in(streams_of[10], 71), 0)
    weights_q = touch_ends(jax.random.randint(streams_of[2], (TOKENS, TOP), 1, 256), jax.random.fold_in(streams_of[2], 1), 1, 255).astype(jnp.int32)
    cotangent = scatter_about(streams_of[3], (TOKENS, D), 1.0, 6.0, ((0, 128),))
    expert_gate = scatter_about(streams_of[4], (EXPERTS * SPLIT, D, HID_DEV), D ** -0.5, 0.0625, ((0, 128),))
    expert_up = scatter_about(streams_of[5], (EXPERTS * SPLIT, D, HID_DEV), D ** -0.5, 0.0625, ((0, 128),))
    expert_down = scatter_about(streams_of[6], (EXPERTS * SPLIT, HID_DEV, D), HID ** -0.5, 0.1875, ((0, 128),))
    shared_gate = scatter_about(streams_of[7], (D, SH_HID), D ** -0.5, 0.0625, ((1, 16),))
    shared_up = scatter_about(streams_of[8], (D, SH_HID), D ** -0.5, 0.0625, ((1, 16),))
    shared_down = scatter_about(streams_of[9], (SH_HID, D), SH_HID ** -0.5, 0.1875, ((0, 16),))
    return {"tokens": tokens, "routes": routes, "weights_q": weights_q, "cotangent": cotangent, "expert_gate": expert_gate, "expert_up": expert_up, "expert_down": expert_down, "shared_gate": shared_gate, "shared_up": shared_up, "shared_down": shared_down}


def silu_grad(values):
    logistic = jax.nn.sigmoid(values)
    return logistic * (1.0 + values * (1.0 - logistic))

def reference(tokens, routes, weights_q, cotangent, expert_gate, expert_up, expert_down, shared_gate, shared_up, shared_down):
    weight = weights_q.astype(jnp.float32) * (1.0 / 256.0)
    slice_count = N_GRP * N_EXP
    most_rows = slice_count * CAP

    def one_slice(carry, index):
        mixed_sum, grad_sum = carry
        expert = index // SPLIT
        matches = routes == expert
        token_weight = lax.optimization_barrier(jnp.sum(jnp.where(matches, weight, 0.0), axis=1))
        named_rows = jnp.any(matches, axis=1)
        row_index = jnp.nonzero(named_rows, size=most_rows, fill_value=0)[0].astype(jnp.int32)
        live_rows = jnp.arange(most_rows, dtype=jnp.int32) < jnp.sum(named_rows.astype(jnp.int32))
        gate_w = lax.dynamic_index_in_dim(expert_gate, index, 0, keepdims=False)
        up_w = lax.dynamic_index_in_dim(expert_up, index, 0, keepdims=False)
        down_w = lax.dynamic_index_in_dim(expert_down, index, 0, keepdims=False)
        x_rows = tokens[row_index]
        grad_rows = cotangent[row_index]
        gate_pre = jnp.dot(x_rows, gate_w, preferred_element_type=jnp.float32)
        up_pre = jnp.dot(x_rows, up_w, preferred_element_type=jnp.float32)
        hidden = (jax.nn.silu(gate_pre) * up_pre).astype(jnp.bfloat16)
        expert_out = lax.optimization_barrier(jnp.dot(hidden, down_w, preferred_element_type=jnp.float32).astype(jnp.bfloat16))
        grad_hidden = jnp.dot(grad_rows, down_w.T, preferred_element_type=jnp.float32)
        grad_gate = (grad_hidden * up_pre * silu_grad(gate_pre)).astype(jnp.bfloat16)
        grad_up = (grad_hidden * jax.nn.silu(gate_pre)).astype(jnp.bfloat16)
        expert_back = jnp.dot(grad_gate, gate_w.T, preferred_element_type=jnp.float32) + jnp.dot(grad_up, up_w.T, preferred_element_type=jnp.float32)
        expert_back = lax.optimization_barrier(expert_back.astype(jnp.bfloat16))
        row_scale = jnp.where(live_rows, token_weight[row_index], 0.0)[:, None]
        mixed_sum = mixed_sum.at[row_index].add(row_scale * expert_out.astype(jnp.float32))
        grad_sum = grad_sum.at[row_index].add(row_scale * expert_back.astype(jnp.float32))
        return ((mixed_sum, grad_sum), None)
    zeros = jnp.zeros(tokens.shape, jnp.float32)
    totals, unused = lax.scan(one_slice, (zeros, zeros), jnp.arange(slice_count, dtype=jnp.int32))
    mixed_sum, grad_sum = totals
    slice_width = SH_HID // N_EXP
    for member in range(N_EXP):
        col_start = member * slice_width
        gate_part = shared_gate[:, col_start:col_start + slice_width]
        up_part = shared_up[:, col_start:col_start + slice_width]
        down_part = shared_down[col_start:col_start + slice_width, :]
        gate_pre = jnp.dot(tokens, gate_part, preferred_element_type=jnp.float32)
        up_pre = jnp.dot(tokens, up_part, preferred_element_type=jnp.float32)
        hidden = (jax.nn.silu(gate_pre) * up_pre).astype(jnp.bfloat16)
        shared_out = lax.optimization_barrier(jnp.dot(hidden, down_part, preferred_element_type=jnp.float32).astype(jnp.bfloat16))
        grad_hidden = jnp.dot(cotangent, down_part.T, preferred_element_type=jnp.float32)
        grad_gate = (grad_hidden * up_pre * silu_grad(gate_pre)).astype(jnp.bfloat16)
        grad_up = (grad_hidden * jax.nn.silu(gate_pre)).astype(jnp.bfloat16)
        shared_back = jnp.dot(grad_gate, gate_part.T, preferred_element_type=jnp.float32) + jnp.dot(grad_up, up_part.T, preferred_element_type=jnp.float32)
        shared_back = lax.optimization_barrier(shared_back.astype(jnp.bfloat16))
        mixed_sum = mixed_sum + shared_out.astype(jnp.float32)
        grad_sum = grad_sum + shared_back.astype(jnp.float32)
    return (mixed_sum.astype(jnp.bfloat16), grad_sum.astype(jnp.bfloat16))
```

```python
import jax
import jax.numpy as jnp
from jax import lax
from jax.sharding import PartitionSpec as P

SPLIT = 2
TOP = 8
CAP = 2
N_Y, N_CORE, N_X, N_Z = 4, 2, 4, 4
INFO = 128

F32, BF16 = jnp.float32, jnp.bfloat16


def silu_parts(values):
    logistic = jax.nn.sigmoid(values)
    return values * logistic, logistic * (1.0 + values * (1.0 - logistic))


def dot(a, b):
    return jnp.dot(a, b, preferred_element_type=F32)


def dot_t(a, b):
    return lax.dot_general(a, b, (((1,), (1,)), ((), ())), preferred_element_type=F32)


def dot_a(a, b):
    return lax.dot_general(a, b, (((0,), (0,)), ((), ())), preferred_element_type=F32)


def move_y(v, k):
    return lax.ppermute(v, "grp", [(y * 2 + c, (y + k) % N_Y * 2 + c) for y in range(N_Y) for c in range(2)])


def swap_core(v):
    return lax.ppermute(v, "grp", [(g, g ^ 1) for g in range(N_Y * 2)])


def move_x(v, k):
    return lax.ppermute(v, "exp", [(x * 4 + z, (x + k) % N_X * 4 + z) for x in range(N_X) for z in range(N_Z)])


def move_z(v, k):
    return lax.ppermute(v, "exp", [(x * 4 + z, x * 4 + (z + k) % N_Z) for x in range(N_X) for z in range(N_Z)])


def ring_gather(move, v):
    return jnp.concatenate([v] + [move(v, k) for k in (1, 2, 3)], axis=0)


def ring_sum(move, parts):
    total = parts[0]
    for k in (1, 2, 3):
        total = total + move(parts[k].astype(BF16), -k).astype(F32)
    return total


def pick(info, experts):
    rows = info.shape[0]
    routes = info[:, :TOP].astype(F32)
    weight = info[:, TOP : 2 * TOP].astype(F32) * (1.0 / 256.0)
    hit = routes[None] == experts.astype(F32)[:, None, None]
    named = jnp.sum(hit.astype(F32), axis=2)
    scale = jnp.sum(jnp.where(hit, weight[None], 0.0), axis=2)
    at = jnp.arange(rows, dtype=jnp.int32)
    earlier = ((at[:, None] // 8 == at[None, :] // 8) & (at[:, None] < at[None, :])).astype(F32)
    rank = dot(named, earlier)
    blocks = jnp.arange(rows // 8, dtype=jnp.int32)
    slots = jnp.arange(CAP, dtype=jnp.int32)
    one_hot = (
        (named[:, None, None, :] > 0.5)
        & (rank[:, None, None, :] == slots.astype(F32)[None, None, :, None])
        & (blocks[None, :, None, None] == (at // 8)[None, None, None, :])
    )
    return one_hot, scale


def local(
    tokens,
    routes,
    weights_q,
    cotangent,
    expert_gate,
    expert_up,
    expert_down,
    shared_gate,
    shared_up,
    shared_down,
):
    width = tokens.shape[1]
    grp, exp = lax.axis_index("grp"), lax.axis_index("exp")
    at_y, at_c, at_x, at_z = grp // 2, grp % 2, exp // 4, exp % 4
    gate_w, up_w, down_w = expert_gate[0], expert_up[0], expert_down[0]
    info = jnp.pad(jnp.concatenate([routes, weights_q], axis=1).astype(BF16), ((0, 0), (0, INFO - 2 * TOP)))

    with jax.named_scope("cot_gather"):
        g_wide = jnp.concatenate([cotangent, info], axis=1)
        g_line = ring_gather(move_y, g_wide)
        g_line = jnp.concatenate([g_line, swap_core(g_line)], axis=0)
        cot_plane = lax.all_gather(cotangent, "exp", axis=0, tiled=True)
    with jax.named_scope("cot_pick"):
        g_experts = grp * 8 + jnp.arange(16, dtype=jnp.int32) // SPLIT
        g_hot, g_scale = pick(g_line[:, width:], g_experts)
        g_hot = g_hot.reshape(16 * 16, 64)
        g_sent = dot(g_hot.astype(BF16), g_line[:, :width]).astype(BF16)
    with jax.named_scope("cot_route"):
        g_rows = lax.all_to_all(g_sent.reshape(16, 16, width), "exp", split_axis=0, concat_axis=0, tiled=True)
        g_rows = g_rows.reshape(256, width)

    with jax.named_scope("tok_gather"):
        x_wide = jnp.concatenate([tokens, info], axis=1)
        x_plane = ring_gather(move_z, ring_gather(move_x, x_wide))
    with jax.named_scope("tok_pick"):
        ky = jnp.arange(8, dtype=jnp.int32) // 2
        cr = jnp.arange(8, dtype=jnp.int32) % 2
        x_experts = ((at_y + ky) % N_Y * 2 + (at_c + cr) % 2) * 8 + exp // SPLIT
        x_hot, x_scale = pick(x_plane[:, width:], x_experts)
        x_hot = x_hot.reshape(8 * 32, 128)
        x_plane = x_plane[:, :width]
        x_sent = dot(x_hot.astype(BF16), x_plane).astype(BF16)
    with jax.named_scope("tok_route"):
        x_sent = x_sent.reshape(4, 64, width)
        x_here = jnp.stack([x_sent[0]] + [move_y(x_sent[k], k) for k in (1, 2, 3)])
        x_here = x_here.reshape(4, 2, 32, width)
        x_rows = jnp.concatenate(
            [x_here[:, 0].reshape(128, width), swap_core(x_here[:, 1].reshape(128, width))], axis=0
        )

    with jax.named_scope("shared"):
        s_gate = dot(x_plane, shared_gate)
        s_up = dot(x_plane, shared_up)
        s_act, s_prime = silu_parts(s_gate)
        shared_out = dot((s_act * s_up).astype(BF16), shared_down)
        s_grad = dot_t(cot_plane, shared_down)
        row = jnp.arange(128, dtype=jnp.int32)
        rel = ((at_z - row // 8 % 4) % 4 * 4 + (at_x - row // 32) % 4) * 8 + row % 8
        to_abs = (rel[:, None] == row[None, :]).astype(F32)
        turn = lambda v: jnp.dot(to_abs, v, precision=lax.Precision.HIGHEST, preferred_element_type=F32)
        s_dg = (s_grad * turn(s_up * s_prime)).astype(BF16)
        s_du = (s_grad * turn(s_act)).astype(BF16)
        shared_back = dot_t(s_dg, shared_gate) + dot_t(s_du, shared_up)
        shared_back = lax.psum_scatter(shared_back.astype(BF16), "exp", scatter_dimension=0, tiled=True)

    with jax.named_scope("expert_fwd"):
        gate_pre = dot(x_rows, gate_w)
        up_pre = dot(x_rows, up_w)
        act, prime = silu_parts(gate_pre)
        y_rows = dot((act * up_pre).astype(BF16), down_w).astype(BF16)
    with jax.named_scope("out_route"):
        y_other = swap_core(y_rows[128:])
        y_mine = jnp.concatenate([y_rows[:128].reshape(4, 32, width), y_other.reshape(4, 32, width)], axis=1)
        y_home = jnp.concatenate([y_mine[0]] + [move_y(y_mine[k], -k) for k in (1, 2, 3)], axis=0)
        x_mix = jnp.where(x_hot.reshape(8, 32, 128), x_scale[:, None, :], 0.0).astype(BF16).reshape(256, 128)
        part = dot_a(x_mix, y_home) + shared_out
        part = ring_sum(move_z, part.reshape(4, 32, width))
        mixed = ring_sum(move_x, part.reshape(4, 8, width)).astype(BF16)
    with jax.named_scope("expert_bwd"):
        slot = jnp.arange(256, dtype=jnp.int32)
        rel = (((at_x - slot // 2 % 4) % 4 * 4 + (at_z - slot // 8 % 4) % 4) * 8 + slot // 32) * 2 + slot % 2
        order = (slot[:, None] == rel[None, :]).astype(F32)
        turn = lambda v: jnp.dot(order, v, precision=lax.Precision.HIGHEST, preferred_element_type=F32)
        grad_hidden = dot_t(g_rows, down_w)
        grad_gate = (grad_hidden * turn(up_pre * prime)).astype(BF16)
        grad_up = (grad_hidden * turn(act)).astype(BF16)
        dx_rows = (dot_t(grad_gate, gate_w) + dot_t(grad_up, up_w)).astype(BF16)
    with jax.named_scope("back_route"):
        dx_home = lax.all_to_all(dx_rows.reshape(16, 16, width), "exp", split_axis=0, concat_axis=0, tiled=True)
        g_mix = jnp.where(g_hot.reshape(16, 16, 64), g_scale[:, None, :], 0.0).astype(BF16).reshape(256, 64)
        part = dot_a(g_mix, dx_home.reshape(256, width))
        part = part[:32] + swap_core(part[32:].astype(BF16)).astype(F32)
        grad = ring_sum(move_y, part.reshape(4, 8, width))
        token_grad = (grad + shared_back.astype(F32)).astype(BF16)
    return (mixed, token_grad)


def solution(mesh):
    in_specs = (
        P(("grp", "exp"), None),
        P(("grp", "exp"), None),
        P(("grp", "exp"), None),
        P(("grp", "exp"), None),
        P(("grp", "exp"), None, None),
        P(("grp", "exp"), None, None),
        P(("grp", "exp"), None, None),
        P(None, "exp"),
        P(None, "exp"),
        P("exp", None),
    )
    out_specs = (P(("grp", "exp"), None), P(("grp", "exp"), None))
    return jax.shard_map(local, mesh=mesh, in_specs=in_specs, out_specs=out_specs, check_vma=False)
```

```python
import functools

import jax
import jax.numpy as jnp
from jax import lax
from jax.experimental import pallas as pl
from jax.experimental.pallas import tpu as pltpu
from jax.sharding import PartitionSpec as P

SPLIT = 2
TOP = 8
CAP = 2
N_Y, N_X, N_Z = 4, 4, 4
INFO = 128
BLK = 1024

F32, BF16, I32 = jnp.float32, jnp.bfloat16, jnp.int32


def silu_parts(values):
    logistic = 1.0 / (1.0 + jnp.exp(-values))
    return values * logistic, logistic * (1.0 + values * (1.0 - logistic))


def dot(a, b):
    return jnp.dot(a, b, preferred_element_type=F32)


def dot_t(a, b):
    return lax.dot_general(a, b, (((1,), (1,)), ((), ())), preferred_element_type=F32)


def dot_a(a, b):
    return lax.dot_general(a, b, (((0,), (0,)), ((), ())), preferred_element_type=F32)


def turn(order, v):
    return jnp.dot(order, v, precision=lax.Precision.HIGHEST, preferred_element_type=F32)


def grid_ids(rows, cols):
    return lax.broadcasted_iota(I32, (rows, cols), 0), lax.broadcasted_iota(I32, (rows, cols), 1)


def move_y(v, k):
    return lax.ppermute(v, "grp", [(y * 2 + c, (y + k) % N_Y * 2 + c) for y in range(N_Y) for c in range(2)])


def swap_core(v):
    return lax.ppermute(v, "grp", [(g, g ^ 1) for g in range(N_Y * 2)])


def move_x(v, k):
    return lax.ppermute(v, "exp", [(x * 4 + z, (x + k) % N_X * 4 + z) for x in range(N_X) for z in range(N_Z)])


def move_z(v, k):
    return lax.ppermute(v, "exp", [(x * 4 + z, x * 4 + (z + k) % N_Z) for x in range(N_X) for z in range(N_Z)])


def ring(move, v):
    return [v] + [move(v, k) for k in (1, 2, 3)]


def ring_sum(move, parts):
    total = parts[0].astype(F32)
    for k in (1, 2, 3):
        total = total + move(parts[k], -k).astype(F32)
    return total


def call(kernel, grid, ins, outs, scratch, flops, moved):
    in_specs = [
        pl.BlockSpec(memory_space=pltpu.SMEM)
        if block == "smem"
        else pl.BlockSpec(memory_space=pl.ANY)
        if block == "any"
        else pl.BlockSpec(block, at)
        for _, block, at in ins
    ]
    return pl.pallas_call(
        kernel,
        grid=(grid,),
        in_specs=in_specs,
        out_specs=[pl.BlockSpec(block, at) for _, _, block, at in outs],
        out_shape=[jax.ShapeDtypeStruct(shape, dtype) for shape, dtype, _, _ in outs],
        scratch_shapes=scratch,
        compiler_params=pltpu.CompilerParams(vmem_limit_bytes=28 * 1024 * 1024),
        cost_estimate=pl.CostEstimate(flops=flops, bytes_accessed=moved, transcendentals=0),
    )(*[a for a, _, _ in ins])


COL = lambda i: (0, i)
FIX = lambda i: (0, 0)


def slots_of(info, expert, block, rank):
    rows = info.shape[0]
    a, b = grid_ids(2 * TOP, INFO)
    across = dot_t((a == b).astype(BF16), info)
    want = expert.astype(F32)
    named = jnp.zeros(expert.shape, F32)
    scale = jnp.zeros(expert.shape, F32)
    for k in range(TOP):
        hit = across[k : k + 1, :] == want
        named = named + jnp.where(hit, 1.0, 0.0)
        scale = scale + jnp.where(hit, across[TOP + k : TOP + k + 1, :], 0.0)
    a, b = grid_ids(rows, rows)
    earlier = jnp.where(((a >> 3) == (b >> 3)) & (a < b), 1.0, 0.0).astype(BF16)
    before = dot(named.astype(BF16), earlier)
    _, row = grid_ids(*expert.shape)
    taken = (named > 0.5) & (before == rank.astype(F32)) & ((row >> 3) == block)
    return jnp.where(taken, 1.0, 0.0).astype(BF16), jnp.where(taken, scale * (1.0 / 256.0), 0.0).astype(BF16)


def cot_pick_kernel(at, g0, g1, i0, i1, sent, mix, hot):
    @pl.when(pl.program_id(0) == 0)
    def _():
        slot, _ = grid_ids(256, 64)
        info = jnp.concatenate([i0[...], i1[...]], axis=0)
        one, scaled = slots_of(info, at[0] * 8 + (slot >> 5), (slot >> 1) & 7, slot & 1)
        hot[...] = one
        mix[...] = scaled

    sent[...] = dot(hot[...], jnp.concatenate([g0[...], g1[...]], axis=0)).astype(BF16)


def tok_pick_kernel(at, _, b0, b1, b2, b3, i0, i1, i2, i3, sg, su, *rest):
    sent, (mix, gate, up, hot, acc) = rest[:8], rest[8:]
    step = pl.program_id(0)

    @pl.when(step == 0)
    def _():
        slot, _ = grid_ids(256, 128)
        info = jnp.concatenate([i0[...], i1[...], i2[...], i3[...]], axis=0)
        y = (at[0] // 2 + (slot >> 6)) & 3
        c = (at[0] + (slot >> 5)) & 1
        one, scaled = slots_of(info, (y * 2 + c) * 8 + at[1] // SPLIT, (slot >> 1) & 15, slot & 1)
        hot[...] = one
        mix[...] = scaled
        acc[...] = jnp.zeros_like(acc)

    rows = jnp.concatenate([b0[...], b1[...], b2[...], b3[...]], axis=0)
    picked = dot(hot[...], rows).astype(BF16)
    for n in range(8):
        sent[n][...] = picked[n * 32 : n * 32 + 32]
    acc[:, :64] += dot(rows, sg[...])
    acc[:, 64:] += dot(rows, su[...])

    @pl.when(step == pl.num_programs(0) - 1)
    def _():
        gate[...] = acc[:, :64]
        up[...] = acc[:, 64:]


def forward_kernel(*refs):
    xs, (gw, uw, dw), ys, (act, slope, acc_g, acc_u, hid) = refs[:8], refs[8:11], refs[11:19], refs[19:]
    step = pl.program_id(0)
    half = pl.num_programs(0) // 2

    @pl.when(step == 0)
    def _():
        acc_g[...] = jnp.zeros_like(acc_g)
        acc_u[...] = jnp.zeros_like(acc_u)

    @pl.when(step < half)
    def _():
        rows = jnp.concatenate([x[...] for x in xs], axis=0)
        acc_g[...] += dot(rows, gw[0])
        acc_u[...] += dot(rows, uw[0])

    @pl.when(step == half - 1)
    def _():
        silu, prime = silu_parts(acc_g[...])
        act[...] = silu
        slope[...] = acc_u[...] * prime
        hid[...] = (silu * acc_u[...]).astype(BF16)

    @pl.when(step >= half)
    def _():
        out = dot(hid[...], dw[0]).astype(BF16)
        for n in range(8):
            ys[n][...] = out[n * 32 : n * 32 + 32]


def grad_hidden_kernel(g, dw, out):
    @pl.when(pl.program_id(0) == 0)
    def _():
        out[...] = jnp.zeros_like(out)

    out[...] += dot_t(g[...], dw[0])


def backward_kernel(at, grad, act, slope, gw, uw, dx, dg, du):
    @pl.when(pl.program_id(0) == 0)
    def _():
        to, i = grid_ids(256, 256)
        x = (at[1] // 4 - ((i >> 1) & 3)) & 3
        z = (at[1] - ((i >> 3) & 3)) & 3
        order = jnp.where(to == ((x * 4 + z) * 8 + (i >> 5)) * 2 + (i & 1), 1.0, 0.0)
        dg[...] = (grad[...] * turn(order, slope[...])).astype(BF16)
        du[...] = (grad[...] * turn(order, act[...])).astype(BF16)

    dx[...] = (dot_t(dg[...], gw[0]) + dot_t(du[...], uw[0])).astype(BF16)


def out_sum_kernel(*refs):
    ys, (mix, gate, up, sd), outs, (hid,) = refs[:8], refs[8:12], refs[12:16], refs[16:]

    @pl.when(pl.program_id(0) == 0)
    def _():
        silu, _ = silu_parts(gate[...])
        hid[...] = (silu * up[...]).astype(BF16)

    rows = jnp.concatenate([y[...] for y in ys], axis=0)
    total = (dot_a(mix[...], rows) + dot(hid[...], sd[...])).astype(BF16)
    for n in range(4):
        outs[n][...] = total[n * 32 : n * 32 + 32]


def back_sum_kernel(rows, mix, mine, other):
    total = dot_a(mix[...], rows[...])
    mine[...] = total[:32]
    other[...] = total[32:].astype(BF16)


def shared_back_kernel(at, g, gate, up, sd, sg, su, o0, o1, o2, o3, acc, dg, du):
    step = pl.program_id(0)
    half = pl.num_programs(0) // 2

    @pl.when(step == 0)
    def _():
        acc[...] = jnp.zeros_like(acc)

    @pl.when(step < half)
    def _():
        acc[...] += dot_t(g[...], sd[...])

    @pl.when(step == half - 1)
    def _():
        to, i = grid_ids(128, 128)
        kx, kz = to >> 5, (to >> 3) & 3
        from_x = jnp.where(i == (kz * 4 + kx) * 8 + (to & 7), 1.0, 0.0)
        x, z = (at[1] // 4 - kx) & 3, (at[1] - kz) & 3
        from_g = jnp.where(i == (x * 4 + z) * 8 + (to & 7), 1.0, 0.0)
        silu, prime = silu_parts(gate[...])
        grad = turn(from_g, acc[...])
        dg[...] = (grad * turn(from_x, up[...] * prime)).astype(BF16)
        du[...] = (grad * turn(from_x, silu)).astype(BF16)

    @pl.when(step >= half)
    def _():
        total = (dot_t(dg[...], sg[...]) + dot_t(du[...], su[...])).astype(BF16)
        o0[...] = total[:32]
        o1[...] = total[32:64]
        o2[...] = total[64:96]
        o3[...] = total[96:]


def local(
    tokens,
    routes,
    weights_q,
    cotangent,
    expert_gate,
    expert_up,
    expert_down,
    shared_gate,
    shared_up,
    shared_down,
):
    width = tokens.shape[1]
    hidden = expert_gate.shape[2]
    part = shared_gate.shape[1]
    steps = width // BLK
    tail = width // INFO
    grp, exp = lax.axis_index("grp"), lax.axis_index("exp")
    at = jnp.stack([grp, exp]).astype(I32)
    info = jnp.pad(jnp.concatenate([routes, weights_q], axis=1).astype(BF16), ((0, 0), (0, INFO - 2 * TOP)))
    first = lambda i: (0, jnp.minimum(i, steps - 1))
    later = lambda i: (0, jnp.maximum(i - steps, 0))
    info_at = lambda i: (0, tail)
    SM = lambda a: (a, "smem", None)

    x_wide = jnp.concatenate([tokens, info], axis=1)
    g_wide = jnp.concatenate([cotangent, info], axis=1)
    with jax.named_scope("tok_gather"):
        x_line = jnp.concatenate(ring(move_x, x_wide), axis=0)
        x_blocks = ring(move_z, x_line)
    with jax.named_scope("cot_gather"):
        g_line = jnp.concatenate(ring(move_y, g_wide), axis=0)
        g_blocks = [g_line, swap_core(g_line)]
        cot_plane = lax.all_gather(cotangent, "exp", axis=0, tiled=True)

    with jax.named_scope("cot_pick"):
        g_sent, g_mix = call(
            cot_pick_kernel,
            steps,
            [SM(at)] + [(b, (32, BLK), COL) for b in g_blocks] + [(b, (32, INFO), info_at) for b in g_blocks],
            [((256, width), BF16, (256, BLK), COL), ((256, 64), BF16, (256, 64), FIX)],
            [pltpu.VMEM((256, 64), BF16)],
            2 * 256 * 64 * width,
            2 * 320 * width,
        )
    with jax.named_scope("cot_route"):
        g_rows = lax.all_to_all(g_sent.reshape(16, 16, width), "exp", split_axis=0, concat_axis=0, tiled=True)
        g_rows = g_rows.reshape(256, width)

    with jax.named_scope("tok_pick"):
        *x_sent, x_mix, s_gate, s_up = call(
            tok_pick_kernel,
            steps,
            [SM(at), (g_mix, "any", None)]
            + [(b, (32, BLK), COL) for b in x_blocks]
            + [(b, (32, INFO), info_at) for b in x_blocks]
            + [(shared_gate, (BLK, part), lambda i: (i, 0)), (shared_up, (BLK, part), lambda i: (i, 0))],
            [((32, width), BF16, (32, BLK), COL)] * 8
            + [((256, 128), BF16, (256, 128), FIX), ((128, part), F32, (128, part), FIX), ((128, part), F32, (128, part), FIX)],
            [pltpu.VMEM((256, 128), BF16), pltpu.VMEM((128, 2 * part), F32)],
            2 * 256 * 128 * width,
            2 * 500 * width,
        )
    with jax.named_scope("tok_route"):
        over = [x_sent[1]] + [move_y(x_sent[2 * k + 1], k) for k in (1, 2, 3)]
        x_rows = [x_sent[0]] + [move_y(x_sent[2 * k], k) for k in (1, 2, 3)]
        x_rows = x_rows + [swap_core(v) for v in over]

    with jax.named_scope("expert_grad_hidden"):
        (grad_hidden,) = call(
            grad_hidden_kernel,
            steps,
            [(g_rows, (256, BLK), COL), (expert_down, (1, hidden, BLK), lambda i: (0, 0, i))],
            [((256, hidden), F32, (256, hidden), FIX)],
            [],
            2 * 256 * hidden * width,
            2 * (256 + hidden) * width,
        )
    with jax.named_scope("expert_forward"):
        up_to = lambda i: (0, jnp.minimum(i, steps - 1), 0)
        *y_rows, act, slope = call(
            forward_kernel,
            2 * steps,
            [(x, (32, BLK), first) for x in x_rows]
            + [
                (expert_gate, (1, BLK, hidden), up_to),
                (expert_up, (1, BLK, hidden), up_to),
                (expert_down, (1, hidden, BLK), lambda i: (0, 0, jnp.maximum(i - steps, 0))),
            ],
            [((32, width), BF16, (32, BLK), later)] * 8 + [((256, hidden), F32, (256, hidden), FIX)] * 2,
            [pltpu.VMEM((256, hidden), F32), pltpu.VMEM((256, hidden), F32), pltpu.VMEM((256, hidden), BF16)],
            6 * 256 * hidden * width,
            2 * (512 + 3 * hidden) * width,
        )
    with jax.named_scope("expert_backward"):
        (dx_rows,) = call(
            backward_kernel,
            steps,
            [
                SM(at),
                (grad_hidden, (256, hidden), FIX),
                (act, (256, hidden), FIX),
                (slope, (256, hidden), FIX),
                (expert_gate, (1, BLK, hidden), lambda i: (0, i, 0)),
                (expert_up, (1, BLK, hidden), lambda i: (0, i, 0)),
            ],
            [((256, width), BF16, (256, BLK), COL)],
            [pltpu.VMEM((256, hidden), BF16), pltpu.VMEM((256, hidden), BF16)],
            4 * 256 * hidden * width,
            2 * (256 + 2 * hidden) * width,
        )
    with jax.named_scope("back_route"):
        dx_home = lax.all_to_all(dx_rows.reshape(16, 16, width), "exp", split_axis=0, concat_axis=0, tiled=True)
        dx_home = dx_home.reshape(256, width)

    with jax.named_scope("out_route"):
        y_other = [swap_core(v) for v in y_rows[4:]]
        y_home = [y_rows[0], y_other[0]]
        for k in (1, 2, 3):
            y_home += [move_y(y_rows[k], -k), move_y(y_other[k], -k)]
        parts = call(
            out_sum_kernel,
            steps,
            [(v, (32, BLK), COL) for v in y_home]
            + [
                (x_mix, (256, 128), FIX),
                (s_gate, (128, part), FIX),
                (s_up, (128, part), FIX),
                (shared_down, (part, BLK), COL),
            ],
            [((32, width), BF16, (32, BLK), COL)] * 4,
            [pltpu.VMEM((128, part), BF16)],
            2 * 256 * 128 * width,
            2 * 400 * width,
        )
        line = ring_sum(move_z, parts).astype(BF16).reshape(4, 8, width)
        mixed = ring_sum(move_x, [line[k] for k in range(4)]).astype(BF16)

    with jax.named_scope("shared_back"):
        twice = lambda i: (0, jnp.where(i < steps, i, 0))
        s_parts = call(
            shared_back_kernel,
            2 * steps,
            [
                SM(at),
                (cot_plane, (128, BLK), first),
                (s_gate, (128, part), FIX),
                (s_up, (128, part), FIX),
                (shared_down, (part, BLK), first),
                (shared_gate, (BLK, part), lambda i: (jnp.maximum(i - steps, 0), 0)),
                (shared_up, (BLK, part), lambda i: (jnp.maximum(i - steps, 0), 0)),
            ],
            [((32, width), BF16, (32, BLK), later)] * 4,
            [pltpu.VMEM((128, part), F32), pltpu.VMEM((128, part), BF16), pltpu.VMEM((128, part), BF16)],
            6 * 128 * part * width,
            2 * 500 * width,
        )
        s_line = ring_sum(move_x, s_parts).astype(BF16).reshape(4, 8, width)
        s_grad = ring_sum(move_z, [s_line[k] for k in range(4)])

    with jax.named_scope("back_sum"):
        mine, other = call(
            back_sum_kernel,
            steps,
            [(dx_home, (256, BLK), COL), (g_mix, (256, 64), FIX)],
            [((32, width), F32, (32, BLK), COL), ((32, width), BF16, (32, BLK), COL)],
            [],
            2 * 256 * 64 * width,
            2 * 352 * width,
        )
        line = (mine + swap_core(other).astype(F32)).reshape(4, 8, width)
        line = [line[0]] + [line[k].astype(BF16) for k in (1, 2, 3)]
        token_grad = (ring_sum(move_y, line) + s_grad).astype(BF16)
    return (mixed, token_grad)


def solution(mesh):
    in_specs = (
        P(("grp", "exp"), None),
        P(("grp", "exp"), None),
        P(("grp", "exp"), None),
        P(("grp", "exp"), None),
        P(("grp", "exp"), None, None),
        P(("grp", "exp"), None, None),
        P(("grp", "exp"), None, None),
        P(None, "exp"),
        P(None, "exp"),
        P("exp", None),
    )
    out_specs = (P(("grp", "exp"), None), P(("grp", "exp"), None))
    return jax.shard_map(local, mesh=mesh, in_specs=in_specs, out_specs=out_specs, check_vma=False)
```

```python
import functools

import jax
import jax.numpy as jnp
from jax import lax
from jax.experimental import pallas as pl
from jax.experimental.pallas import tpu as pltpu
from jax.sharding import PartitionSpec as P

SPLIT = 2
TOP = 8
CAP = 2
N_Y, N_X, N_Z = 4, 4, 4
INFO = 128
BLK = 1792

F32, BF16, I32 = jnp.float32, jnp.bfloat16, jnp.int32


def silu_parts(values):
    logistic = 1.0 / (1.0 + jnp.exp(-values))
    return values * logistic, logistic * (1.0 + values * (1.0 - logistic))


def dot(a, b):
    return jnp.dot(a, b, preferred_element_type=F32)


def dot_t(a, b):
    return lax.dot_general(a, b, (((1,), (1,)), ((), ())), preferred_element_type=F32)


def dot_a(a, b):
    return lax.dot_general(a, b, (((0,), (0,)), ((), ())), preferred_element_type=F32)


def turn(order, v):
    return jnp.dot(order, v, precision=lax.Precision.HIGHEST, preferred_element_type=F32)


def grid_ids(rows, cols):
    return lax.broadcasted_iota(I32, (rows, cols), 0), lax.broadcasted_iota(I32, (rows, cols), 1)


def move_y(v, k):
    return lax.ppermute(v, "grp", [(y * 2 + c, (y + k) % N_Y * 2 + c) for y in range(N_Y) for c in range(2)])


def swap_core(v):
    return lax.ppermute(v, "grp", [(g, g ^ 1) for g in range(N_Y * 2)])


def move_plane(v, k, turned):
    pairs = []
    for grp in range(N_Y * 2):
        for x in range(N_X):
            for z in range(N_Z):
                along_x = (grp % 2 == 0) != turned
                to = (x + k) % N_X * 4 + z if along_x else x * 4 + (z + k) % N_Z
                pairs.append((grp * 16 + x * 4 + z, grp * 16 + to))
    return lax.ppermute(v, ("grp", "exp"), pairs)


def move_a(v, k):
    return move_plane(v, k, False)


def move_b(v, k):
    return move_plane(v, k, True)


def ring(move, v):
    return [v] + [move(v, k) for k in (1, 2, 3)]


def ring_sum(move, parts):
    total = parts[0].astype(F32)
    for k in (1, 2, 3):
        total = total + move(parts[k], -k).astype(F32)
    return total


def call(kernel, grid, ins, outs, scratch, flops, moved, after=()):
    in_specs = [pl.BlockSpec(memory_space=pl.ANY)] * len(after) + [
        pl.BlockSpec(memory_space=pltpu.SMEM) if block == "smem" else pl.BlockSpec(block, at) for _, block, at in ins
    ]
    skip = len(after)
    return pl.pallas_call(
        lambda *refs: kernel(*refs[skip:]),
        grid=(grid,),
        in_specs=in_specs,
        out_specs=[pl.BlockSpec(block, at) for _, _, block, at in outs],
        out_shape=[jax.ShapeDtypeStruct(shape, dtype) for shape, dtype, _, _ in outs],
        scratch_shapes=scratch,
        compiler_params=pltpu.CompilerParams(vmem_limit_bytes=60 * 1024 * 1024),
        cost_estimate=pl.CostEstimate(flops=flops, bytes_accessed=moved, transcendentals=0),
    )(*after, *[a for a, _, _ in ins])


COL = lambda i: (0, i)
FIX = lambda i: (0, 0)


def slots_of(info, expert, block, rank):
    rows = info.shape[0]
    a, b = grid_ids(2 * TOP, INFO)
    across = dot_t((a == b).astype(BF16), info)
    want = expert.astype(F32)
    named = jnp.zeros(expert.shape, F32)
    scale = jnp.zeros(expert.shape, F32)
    for k in range(TOP):
        hit = across[k : k + 1, :] == want
        named = named + jnp.where(hit, 1.0, 0.0)
        scale = scale + jnp.where(hit, across[TOP + k : TOP + k + 1, :], 0.0)
    a, b = grid_ids(rows, rows)
    earlier = jnp.where(((a >> 3) == (b >> 3)) & (a < b), 1.0, 0.0).astype(BF16)
    before = dot(named.astype(BF16), earlier)
    _, row = grid_ids(*expert.shape)
    taken = (named > 0.5) & (before == rank.astype(F32)) & ((row >> 3) == block)
    return jnp.where(taken, 1.0, 0.0).astype(BF16), jnp.where(taken, scale * (1.0 / 256.0), 0.0).astype(BF16)


def cot_pick_kernel(at, g0, g1, i0, i1, sent, mix, hot):
    @pl.when(pl.program_id(0) == 0)
    def _():
        slot, _ = grid_ids(256, 64)
        info = jnp.concatenate([i0[...], i1[...]], axis=0)
        one, scaled = slots_of(info, at[0] * 8 + (slot >> 5), (slot >> 1) & 7, slot & 1)
        hot[...] = one
        mix[...] = scaled

    sent[...] = dot(hot[...], jnp.concatenate([g0[...], g1[...]], axis=0)).astype(BF16)


def widen_kernel(tok, cot, routes, weights, all_, g):
    width = tok.shape[1]
    at, to = grid_ids(TOP, INFO)
    place = lambda v, n: dot(v.astype(F32).astype(BF16), jnp.where(to == at + n, 1.0, 0.0).astype(BF16))
    info = (place(routes[...], 0) + place(weights[...], TOP)).astype(BF16)
    all_[:, :width] = cot[...]
    all_[:, width : 2 * width] = tok[...]
    all_[:, 2 * width :] = info
    g[:, :width] = cot[...]
    g[:, width:] = info


def tok_pick_kernel(at, b0, b1, b2, b3, i0, i1, i2, i3, *rest):
    sent, (over, mix, hot) = rest[:4], rest[4:]

    @pl.when(pl.program_id(0) == 0)
    def _():
        slot, _ = grid_ids(256, 128)
        info = jnp.concatenate([i0[...], i1[...], i2[...], i3[...]], axis=0)
        y = (at[0] // 2 + (slot >> 5)) & 3
        c = (at[0] + (slot >> 7)) & 1
        one, scaled = slots_of(info, (y * 2 + c) * 8 + at[1] // SPLIT, (slot >> 1) & 15, slot & 1)
        hot[...] = one
        mix[...] = scaled

    picked = dot(hot[...], jnp.concatenate([b0[...], b1[...], b2[...], b3[...]], axis=0)).astype(BF16)
    for n in range(4):
        sent[n][...] = picked[n * 32 : n * 32 + 32]
    over[...] = picked[128:]


def order_of(at):
    to, i = grid_ids(256, 256)
    from_1 = ((at[0] + (i >> 7)) & 1) == 1
    inner, outer = (i >> 1) & 3, (i >> 3) & 3
    x = (at[1] // 4 - jnp.where(from_1, outer, inner)) & 3
    z = (at[1] - jnp.where(from_1, inner, outer)) & 3
    return jnp.where(to == ((x * 4 + z) * 8 + (i >> 5)) * 2 + (i & 1), 1.0, 0.0)


def forward_kernel(at, *refs):
    xs, (gw, uw, hid, act, slope, acc_g, acc_u) = refs[:8], refs[8:]
    step = pl.program_id(0)

    @pl.when(step == 0)
    def _():
        acc_g[...] = jnp.zeros_like(acc_g)
        acc_u[...] = jnp.zeros_like(acc_u)

    rows = jnp.concatenate([x[...] for x in xs], axis=0)
    acc_g[...] += dot(rows, gw[0])
    acc_u[...] += dot(rows, uw[0])

    @pl.when(step == pl.num_programs(0) - 1)
    def _():
        silu, prime = silu_parts(acc_g[...])
        act[...] = silu
        slope[...] = acc_u[...] * prime
        hid[...] = dot(order_of(at).astype(BF16), (silu * acc_u[...]).astype(BF16)).astype(BF16)


def grad_kernel(at, g, dw, act, slope, dg, du, acc):
    step = pl.program_id(0)

    @pl.when(step == 0)
    def _():
        acc[...] = jnp.zeros_like(acc)

    acc[...] += dot_t(g[...], dw[0])

    @pl.when(step == pl.num_programs(0) - 1)
    def _():
        grad = lax.dot_general(
            order_of(at), acc[...], (((0,), (0,)), ((), ())), precision=lax.Precision.HIGHEST, preferred_element_type=F32
        )
        dg[...] = (grad * slope[...]).astype(BF16)
        du[...] = (grad * act[...]).astype(BF16)


def backward_kernel(dg, du, hid, gw, uw, dw, *outs):
    dx = (dot_t(dg[...], gw[0]) + dot_t(du[...], uw[0])).astype(BF16)
    for n in range(4):
        outs[n][...] = dx[n * 32 : n * 32 + 32]
    outs[4][...] = dx[128:]
    outs[5][...] = dot(hid[...], dw[0]).astype(BF16)


def back_sum_kernel(*refs):
    blocks, (mix, hid, grads, sg, su, sd), outs = refs[:8], refs[8:14], refs[14:]
    step = pl.program_id(0)
    half = pl.num_programs(0) // 2

    def put(total):
        for n in range(4):
            outs[n][...] = total[n * 32 : n * 32 + 32].astype(BF16)

    @pl.when(step < half)
    def _():
        rows = jnp.concatenate([v[...] for v in blocks], axis=0)
        put(dot_a(mix[...], rows) + dot(grads[...], jnp.concatenate([sg[...], su[...]], axis=0)))

    @pl.when(step >= half)
    def _():
        put(dot(hid[...], sd[...]))


def out_sum_kernel(rows, mix, mine, other):
    total = dot_a(mix[...], rows[...])
    mine[...] = total[:32]
    other[...] = total[32:].astype(BF16)


def shared_kernel(*refs):
    xs, gs, (sg, su, sd), (hid, grads, acc, acc_g) = refs[:4], refs[4:8], refs[8:11], refs[11:]
    step = pl.program_id(0)
    part = sg.shape[0]

    @pl.when(step == 0)
    def _():
        acc[...] = jnp.zeros_like(acc)
        acc_g[...] = jnp.zeros_like(acc_g)

    rows = jnp.concatenate([x[...] for x in xs], axis=0)
    acc[...] += dot_t(rows, jnp.concatenate([sg[...], su[...]], axis=0))
    acc_g[...] += dot_t(jnp.concatenate([g[...] for g in gs], axis=0), sd[...])

    @pl.when(step == pl.num_programs(0) - 1)
    def _():
        up = acc[:, part:]
        silu, prime = silu_parts(acc[:, :part])
        hid[...] = (silu * up).astype(BF16)
        grads[:, :part] = (acc_g[...] * up * prime).astype(BF16)
        grads[:, part:] = (acc_g[...] * silu).astype(BF16)


def local(
    tokens,
    routes,
    weights_q,
    cotangent,
    expert_gate,
    expert_up,
    expert_down,
    shared_gate,
    shared_up,
    shared_down,
):
    width = tokens.shape[1]
    hidden = expert_gate.shape[2]
    part = shared_gate.shape[1]
    steps = width // BLK
    tail = width // INFO
    grp, exp = lax.axis_index("grp"), lax.axis_index("exp")
    at = jnp.stack([grp, exp]).astype(I32)
    info = jnp.pad(jnp.concatenate([routes, weights_q], axis=1).astype(BF16), ((0, 0), (0, INFO - 2 * TOP)))
    first = lambda i: (0, jnp.minimum(i, steps - 1))
    later = lambda i: (0, jnp.maximum(i - steps, 0))
    info_at = lambda i: (0, tail)
    SM = lambda a: (a, "smem", None)

    with jax.named_scope("widen"):
        whole = lambda v: (v, v.shape, FIX)
        made = lambda rows, cols: ((rows, cols), BF16, (rows, cols), FIX)
        all_wide, g_wide = call(
            widen_kernel,
            1,
            [whole(v) for v in (tokens, cotangent, routes, weights_q)],
            [made(8, 2 * width + INFO), made(8, width + INFO)],
            [],
            0,
            4 * width * 16,
        )
    with jax.named_scope("gather_line"):
        all_line = ring(move_a, all_wide)
    with jax.named_scope("gather_plane"):
        plane = ring(move_b, jnp.concatenate(all_line, axis=0))
    with jax.named_scope("cot_gather"):
        g_line = jnp.concatenate(ring(move_y, g_wide), axis=0)
        g_blocks = [g_line, swap_core(g_line)]

    with jax.named_scope("cot_pick"):
        g_sent, g_mix = call(
            cot_pick_kernel,
            steps,
            [SM(at)] + [(b, (32, BLK), COL) for b in g_blocks] + [(b, (32, INFO), info_at) for b in g_blocks],
            [((256, width), BF16, (256, BLK), COL), ((256, 64), BF16, (256, 64), FIX)],
            [pltpu.VMEM((256, 64), BF16)],
            2 * 256 * 64 * width,
            2 * 320 * width,
        )
    with jax.named_scope("cot_route"):
        g_rows = lax.all_to_all(g_sent.reshape(16, 16, width), "exp", split_axis=0, concat_axis=0, tiled=True)
        g_rows = g_rows.reshape(256, width)

    with jax.named_scope("tok_pick"):
        *x_sent, x_over, x_mix = call(
            tok_pick_kernel,
            steps,
            [SM(at)]
            + [(b, (32, BLK), lambda i: (0, steps + i)) for b in plane]
            + [(b, (32, INFO), lambda i: (0, 2 * tail)) for b in plane],
            [((32, width), BF16, (32, BLK), COL)] * 4
            + [((128, width), BF16, (128, BLK), COL), ((256, 128), BF16, (256, 128), FIX)],
            [pltpu.VMEM((256, 128), BF16)],
            2 * 256 * 128 * width,
            2 * 400 * width,
            after=[g_mix],
        )
    with jax.named_scope("tok_route"):
        x_rows = [x_sent[0]] + [move_y(x_sent[k], k) for k in (1, 2, 3)]
        x_over = swap_core(x_over)
        x_over = [x_over[k * 32 : k * 32 + 32] for k in range(4)]
        x_rows += [x_over[0]] + [move_y(x_over[k], k) for k in (1, 2, 3)]

    with jax.named_scope("shared"):
        s_hid, s_grads = call(
            shared_kernel,
            steps,
            [(v, (32, BLK), lambda i: (0, steps + i)) for v in plane]
            + [(v, (32, BLK), COL) for v in plane]
            + [(shared_gate.T, (part, BLK), COL), (shared_up.T, (part, BLK), COL), (shared_down, (part, BLK), COL)],
            [((128, part), BF16, (128, part), FIX), ((128, 2 * part), BF16, (128, 2 * part), FIX)],
            [pltpu.VMEM((128, 2 * part), F32), pltpu.VMEM((128, part), F32)],
            6 * 128 * part * width,
            2 * 450 * width,
            after=[x_mix],
        )

    row_at = lambda i: (0, i, 0)
    col_at = lambda i: (0, 0, i)
    pre = ((256, hidden), F32, (256, hidden), FIX)
    mid = ((256, hidden), BF16, (256, hidden), FIX)
    with jax.named_scope("expert_forward"):
        hid, act, slope = call(
            forward_kernel,
            steps,
            [SM(at)]
            + [(x, (32, BLK), COL) for x in x_rows]
            + [(expert_gate, (1, BLK, hidden), row_at), (expert_up, (1, BLK, hidden), row_at)],
            [mid, pre, pre],
            [pltpu.VMEM((256, hidden), F32), pltpu.VMEM((256, hidden), F32)],
            4 * 256 * hidden * width,
            2 * (256 + 2 * hidden) * width,
            after=[s_hid],
        )
    with jax.named_scope("expert_grad"):
        dg, du = call(
            grad_kernel,
            steps,
            [
                SM(at),
                (g_rows, (256, BLK), COL),
                (expert_down, (1, hidden, BLK), col_at),
                (act, (256, hidden), FIX),
                (slope, (256, hidden), FIX),
            ],
            [mid, mid],
            [pltpu.VMEM((256, hidden), F32)],
            2 * 256 * hidden * width,
            2 * (256 + hidden) * width,
        )
    with jax.named_scope("expert_backward"):
        *dx_rows, dx_over, y_rows = call(
            backward_kernel,
            steps,
            [
                (dg, (256, hidden), FIX),
                (du, (256, hidden), FIX),
                (hid, (256, hidden), FIX),
                (expert_gate, (1, BLK, hidden), row_at),
                (expert_up, (1, BLK, hidden), row_at),
                (expert_down, (1, hidden, BLK), col_at),
            ],
            [((32, width), BF16, (32, BLK), COL)] * 4
            + [((128, width), BF16, (128, BLK), COL), ((256, width), BF16, (256, BLK), COL)],
            [],
            6 * 256 * hidden * width,
            2 * (512 + 3 * hidden) * width,
        )
    with jax.named_scope("out_route"):
        y_home = lax.all_to_all(y_rows.reshape(16, 16, width), "exp", split_axis=0, concat_axis=0, tiled=True)
        y_home = y_home.reshape(256, width)

    with jax.named_scope("back_route"):
        dx_home = [dx_rows[0]] + [move_y(dx_rows[k], -k) for k in (1, 2, 3)]
        dx_over = swap_core(dx_over)
        dx_over = [dx_over[k * 32 : k * 32 + 32] for k in range(4)]
        dx_home += [dx_over[0]] + [move_y(dx_over[k], -k) for k in (1, 2, 3)]
        parts = call(
            back_sum_kernel,
            2 * steps,
            [(v, (32, BLK), first) for v in dx_home]
            + [
                (x_mix, (256, 128), FIX),
                (s_hid, (128, part), FIX),
                (s_grads, (128, 2 * part), FIX),
                (shared_gate.T, (part, BLK), first),
                (shared_up.T, (part, BLK), first),
                (shared_down, (part, BLK), later),
            ],
            [((32, 2 * width), BF16, (32, BLK), COL)] * 4,
            [],
            2 * 256 * 128 * width,
            2 * 400 * width,
            after=[y_home],
        )
        line = ring_sum(move_b, parts).astype(BF16).reshape(4, 8, 2 * width)
        both = ring_sum(move_a, [line[k] for k in range(4)])
        token_grad, s_out = both[:, :width].astype(BF16), both[:, width:]
    with jax.named_scope("out_sum"):
        mine, other = call(
            out_sum_kernel,
            steps,
            [(y_home, (256, BLK), COL), (g_mix, (256, 64), FIX)],
            [((32, width), F32, (32, BLK), COL), ((32, width), BF16, (32, BLK), COL)],
            [],
            2 * 256 * 64 * width,
            2 * 352 * width,
        )
        line = (mine + swap_core(other).astype(F32)).reshape(4, 8, width)
        line = [line[0]] + [line[k].astype(BF16) for k in (1, 2, 3)]
        mixed = (ring_sum(move_y, line) + s_out).astype(BF16)
    return (mixed, token_grad)


def solution(mesh):
    in_specs = (
        P(("grp", "exp"), None),
        P(("grp", "exp"), None),
        P(("grp", "exp"), None),
        P(("grp", "exp"), None),
        P(("grp", "exp"), None, None),
        P(("grp", "exp"), None, None),
        P(("grp", "exp"), None, None),
        P(None, "exp"),
        P(None, "exp"),
        P("exp", None),
    )
    out_specs = (P(("grp", "exp"), None), P(("grp", "exp"), None))
    return jax.shard_map(local, mesh=mesh, in_specs=in_specs, out_specs=out_specs, check_vma=False)
```

```python
import functools

import jax
import jax.numpy as jnp
from jax import lax
from jax.experimental import pallas as pl
from jax.experimental.pallas import tpu as pltpu
from jax.sharding import PartitionSpec as P

SPLIT = 2
TOP = 8
CAP = 2
N_Y, N_X, N_Z = 4, 4, 4
INFO = 128
BLK = 3584
CHUNK = 1792

F32, BF16, I32 = jnp.float32, jnp.bfloat16, jnp.int32


def silu_parts(values):
    logistic = 1.0 / (1.0 + jnp.exp(-values))
    return values * logistic, logistic * (1.0 + values * (1.0 - logistic))


def dot(a, b):
    return jnp.dot(a, b, preferred_element_type=F32)


def dot_t(a, b):
    return lax.dot_general(a, b, (((1,), (1,)), ((), ())), preferred_element_type=F32)


def dot_a(a, b):
    return lax.dot_general(a, b, (((0,), (0,)), ((), ())), preferred_element_type=F32)


def turn(order, v):
    return jnp.dot(order, v, precision=lax.Precision.HIGHEST, preferred_element_type=F32)


def grid_ids(rows, cols):
    return lax.broadcasted_iota(I32, (rows, cols), 0), lax.broadcasted_iota(I32, (rows, cols), 1)


def move_y(v, k):
    return lax.ppermute(v, "grp", [(y * 2 + c, (y + k) % N_Y * 2 + c) for y in range(N_Y) for c in range(2)])


def move_y_apart(v):
    return lax.ppermute(v, "grp", [(y * 2 + c, (y + 1 - 2 * c) % N_Y * 2 + c) for y in range(N_Y) for c in range(2)])


def swap_core(v):
    return lax.ppermute(v, "grp", [(g, g ^ 1) for g in range(N_Y * 2)])


def move_plane(v, k, turned):
    pairs = []
    for grp in range(N_Y * 2):
        for x in range(N_X):
            for z in range(N_Z):
                along_x = (grp % 2 == 0) != turned
                to = (x + k) % N_X * 4 + z if along_x else x * 4 + (z + k) % N_Z
                pairs.append((grp * 16 + x * 4 + z, grp * 16 + to))
    return lax.ppermute(v, ("grp", "exp"), pairs)


def move_a(v, k):
    return move_plane(v, k, False)


def move_b(v, k):
    return move_plane(v, k, True)


def ring(move, v):
    return [v] + [move(v, k) for k in (1, 2, 3)]


def ring_sum(move, parts):
    total = parts[0].astype(F32)
    for k in (1, 2, 3):
        total = total + move(parts[k], -k).astype(F32)
    return total


def call(kernel, grid, ins, outs, scratch, flops, moved, after=()):
    in_specs = [pl.BlockSpec(memory_space=pl.ANY)] * len(after) + [
        pl.BlockSpec(memory_space=pltpu.SMEM) if block == "smem" else pl.BlockSpec(block, at) for _, block, at in ins
    ]
    skip = len(after)
    return pl.pallas_call(
        lambda *refs: kernel(*refs[skip:]),
        grid=(grid,),
        in_specs=in_specs,
        out_specs=[pl.BlockSpec(block, at) for _, _, block, at in outs],
        out_shape=[jax.ShapeDtypeStruct(shape, dtype) for shape, dtype, _, _ in outs],
        scratch_shapes=scratch,
        compiler_params=pltpu.CompilerParams(vmem_limit_bytes=60 * 1024 * 1024),
        cost_estimate=pl.CostEstimate(flops=flops, bytes_accessed=moved, transcendentals=0),
    )(*after, *[a for a, _, _ in ins])


COL = lambda i: (0, i)
FIX = lambda i: (0, 0)


def slots_of(info, expert, block, rank):
    rows = info.shape[0]
    a, b = grid_ids(2 * TOP, INFO)
    across = dot_t((a == b).astype(BF16), info)
    want = expert.astype(F32)
    named = jnp.zeros(expert.shape, F32)
    scale = jnp.zeros(expert.shape, F32)
    for k in range(TOP):
        hit = across[k : k + 1, :] == want
        named = named + jnp.where(hit, 1.0, 0.0)
        scale = scale + jnp.where(hit, across[TOP + k : TOP + k + 1, :], 0.0)
    a, b = grid_ids(rows, rows)
    earlier = jnp.where(((a >> 3) == (b >> 3)) & (a < b), 1.0, 0.0).astype(BF16)
    before = dot(named.astype(BF16), earlier)
    _, row = grid_ids(*expert.shape)
    taken = (named > 0.5) & (before == rank.astype(F32)) & ((row >> 3) == block)
    return jnp.where(taken, 1.0, 0.0).astype(BF16), jnp.where(taken, scale * (1.0 / 256.0), 0.0).astype(BF16)


def cot_pick_kernel(at, g0, g1, g2, i0, i1, i2, sent, mix, hot):
    @pl.when(pl.program_id(0) == 0)
    def _():
        slot, _ = grid_ids(256, 64)
        to, i = grid_ids(64, 64)
        near = 1 + 2 * (at[0] & 1)
        far_near = 4 - near
        came = jnp.zeros((64, 64), I32)
        for n, block in enumerate((0, 4, near, 4 + near, 2, 4 + far_near, far_near, 6)):
            came = jnp.where((i >> 3) == n, block, came)
        order = jnp.where(((to >> 3) == came) & ((to & 7) == (i & 7)), 1.0, 0.0).astype(BF16)
        info = jnp.concatenate([i0[...], i1[...], i2[...]], axis=0)
        one, scaled = slots_of(dot(order, info).astype(BF16), at[0] * 8 + (slot >> 5), (slot >> 1) & 7, slot & 1)
        hot[...] = dot(one, order).astype(BF16)
        mix[...] = scaled

    sent[...] = dot(hot[...], jnp.concatenate([g0[...], g1[...], g2[...]], axis=0)).astype(BF16)


def widen_kernel(tok, cot, routes, weights, all_, g):
    width = tok.shape[1]
    at, to = grid_ids(TOP, INFO)
    place = lambda v, n: dot(v.astype(F32).astype(BF16), jnp.where(to == at + n, 1.0, 0.0).astype(BF16))
    info = (place(routes[...], 0) + place(weights[...], TOP)).astype(BF16)
    all_[:, :width] = cot[...]
    all_[:, width : 2 * width] = tok[...]
    all_[:, 2 * width :] = info
    g[:, :width] = cot[...]
    g[:, width:] = info


def tok_pick_kernel(at, b0, b1, b2, b3, i0, i1, i2, i3, *rest):
    sent, (over, mix, hot) = rest[:4], rest[4:]

    @pl.when(pl.program_id(0) == 0)
    def _():
        slot, _ = grid_ids(256, 128)
        info = jnp.concatenate([i0[...], i1[...], i2[...], i3[...]], axis=0)
        y = (at[0] // 2 + (slot >> 5)) & 3
        c = (at[0] + (slot >> 7)) & 1
        one, scaled = slots_of(info, (y * 2 + c) * 8 + at[1] // SPLIT, (slot >> 1) & 15, slot & 1)
        hot[...] = one
        mix[...] = scaled

    picked = dot(hot[...], jnp.concatenate([b0[...], b1[...], b2[...], b3[...]], axis=0)).astype(BF16)
    for n in range(4):
        sent[n][...] = picked[n * 32 : n * 32 + 32]
    over[...] = picked[128:]


def order_of(at):
    to, i = grid_ids(256, 256)
    from_1 = ((at[0] + (i >> 7)) & 1) == 1
    inner, outer = (i >> 1) & 3, (i >> 3) & 3
    x = (at[1] // 4 - jnp.where(from_1, outer, inner)) & 3
    z = (at[1] - jnp.where(from_1, inner, outer)) & 3
    return jnp.where(to == ((x * 4 + z) * 8 + (i >> 5)) * 2 + (i & 1), 1.0, 0.0)


def expert_kernel(at, *refs):
    xs, (g_hbm, gw, uw, dw), dxs, (y_hbm,), (x, g, wg, wu, wd, y, dx, sem, sem_w, sem_o) = (
        refs[:8],
        refs[8:12],
        refs[12:17],
        refs[17:18],
        refs[18:],
    )
    chunks, blk, hidden = wg.shape
    cols = lambda c: pl.ds(pl.multiple_of(c * blk, blk), blk)
    load_x = [pltpu.make_async_copy(v, x.at[pl.ds(n * 32, 32)], sem.at[n]) for n, v in enumerate(xs)]
    load_g = pltpu.make_async_copy(g_hbm, g, sem.at[8])
    load_1 = lambda c: pltpu.make_async_copy(gw.at[0, pl.ds(c * blk, blk)], wg.at[c], sem_w.at[0, c])
    load_2 = lambda c: pltpu.make_async_copy(uw.at[0, pl.ds(c * blk, blk)], wu.at[c], sem_w.at[1, c])
    load_3 = lambda c: pltpu.make_async_copy(dw.at[0, :, cols(c)], wd.at[c], sem_w.at[2, c])
    send_y = lambda c: pltpu.make_async_copy(y.at[:, cols(c)], y_hbm.at[:, cols(c)], sem_o.at[0, c])
    send_dx = [pltpu.make_async_copy(dx.at[pl.ds(n * 32, 32)], v, sem.at[9 + n]) for n, v in enumerate(dxs[:4])]
    send_dx.append(pltpu.make_async_copy(dx.at[pl.ds(128, 128)], dxs[4], sem.at[13]))

    for copy in load_x:
        copy.start()
    for c in range(chunks):
        load_1(c).start()
        load_2(c).start()
    load_g.start()
    for c in range(chunks):
        load_3(c).start()
    for copy in load_x:
        copy.wait()

    def pre(c, accs):
        load_1(c).wait()
        load_2(c).wait()
        rows = x[:, cols(c)]
        return accs[0] + dot(rows, wg[c]), accs[1] + dot(rows, wu[c])

    zero = jnp.zeros((256, hidden), F32)
    gate, up = lax.fori_loop(0, chunks, pre, (zero, zero))
    silu, prime = silu_parts(gate)
    order = order_of(at)
    hid = dot(order.astype(BF16), (silu * up).astype(BF16)).astype(BF16)
    load_g.wait()

    def mid(c, acc):
        load_3(c).wait()
        y[:, cols(c)] = dot(hid, wd[c]).astype(BF16)
        send_y(c).start()
        return acc + dot_t(g[:, cols(c)], wd[c])

    grad = lax.fori_loop(0, chunks, mid, zero)
    grad = lax.dot_general(order, grad, (((0,), (0,)), ((), ())), precision=lax.Precision.HIGHEST, preferred_element_type=F32)
    dg = (grad * (up * prime)).astype(BF16)
    du = (grad * silu).astype(BF16)

    def back(c, _):
        dx[:, cols(c)] = (dot_t(dg, wg[c]) + dot_t(du, wu[c])).astype(BF16)
        return 0

    lax.fori_loop(0, chunks, back, 0)
    for copy in send_dx:
        copy.start()
    for c in range(chunks):
        send_y(c).wait()
    for copy in send_dx:
        copy.wait()


def back_sum_kernel(*refs):
    blocks, (mix, hid, grads, sg, su, sd), outs = refs[:8], refs[8:14], refs[14:]
    step = pl.program_id(0)
    half = pl.num_programs(0) // 2

    def put(total):
        for n in range(4):
            outs[n][...] = total[n * 32 : n * 32 + 32].astype(BF16)

    @pl.when(step < half)
    def _():
        put(dot(hid[...], sd[...]))

    @pl.when(step >= half)
    def _():
        rows = jnp.concatenate([v[...] for v in blocks], axis=0)
        put(dot_a(mix[...], rows) + dot(grads[...], jnp.concatenate([sg[...], su[...]], axis=0)))


def out_sum_kernel(rows, mix, mine, other):
    total = dot_a(mix[...], rows[...])
    mine[...] = total[:32]
    other[...] = total[32:].astype(BF16)


def shared_kernel(*refs):
    xs, gs, (sg, su, sd), (hid, grads, acc, acc_g) = refs[:4], refs[4:8], refs[8:11], refs[11:]
    step = pl.program_id(0)
    part = sg.shape[0]

    @pl.when(step == 0)
    def _():
        acc[...] = jnp.zeros_like(acc)
        acc_g[...] = jnp.zeros_like(acc_g)

    rows = jnp.concatenate([x[...] for x in xs], axis=0)
    acc[...] += dot_t(rows, jnp.concatenate([sg[...], su[...]], axis=0))
    acc_g[...] += dot_t(jnp.concatenate([g[...] for g in gs], axis=0), sd[...])

    @pl.when(step == pl.num_programs(0) - 1)
    def _():
        up = acc[:, part:]
        silu, prime = silu_parts(acc[:, :part])
        hid[...] = (silu * up).astype(BF16)
        grads[:, :part] = (acc_g[...] * up * prime).astype(BF16)
        grads[:, part:] = (acc_g[...] * silu).astype(BF16)


def local(
    tokens,
    routes,
    weights_q,
    cotangent,
    expert_gate,
    expert_up,
    expert_down,
    shared_gate,
    shared_up,
    shared_down,
):
    width = tokens.shape[1]
    hidden = expert_gate.shape[2]
    part = shared_gate.shape[1]
    steps = width // BLK
    tail = width // INFO
    grp, exp = lax.axis_index("grp"), lax.axis_index("exp")
    at = jnp.stack([grp, exp]).astype(I32)
    info = jnp.pad(jnp.concatenate([routes, weights_q], axis=1).astype(BF16), ((0, 0), (0, INFO - 2 * TOP)))
    first = lambda i: (0, jnp.minimum(i, steps - 1))
    later = lambda i: (0, jnp.maximum(i - steps, 0))
    info_at = lambda i: (0, tail)
    SM = lambda a: (a, "smem", None)

    with jax.named_scope("widen"):
        whole = lambda v: (v, v.shape, FIX)
        made = lambda rows, cols: ((rows, cols), BF16, (rows, cols), FIX)
        all_wide, g_wide = call(
            widen_kernel,
            1,
            [whole(v) for v in (tokens, cotangent, routes, weights_q)],
            [made(8, 2 * width + INFO), made(8, width + INFO)],
            [],
            0,
            4 * width * 16,
        )
    with jax.named_scope("gather_line"):
        all_line = ring(move_a, all_wide)
    with jax.named_scope("gather_plane"):
        plane = ring(move_b, jnp.concatenate(all_line, axis=0))
    with jax.named_scope("cot_gather"):
        g_chip = jnp.concatenate([g_wide, swap_core(g_wide)], axis=0)
        g_half = jnp.concatenate([move_y_apart(g_chip), move_y(g_wide, 2)], axis=0)
        g_blocks = [g_chip, g_half, swap_core(g_half)]

    with jax.named_scope("cot_pick"):
        g_sent, g_mix = call(
            cot_pick_kernel,
            steps,
            [SM(at)]
            + [(b, (b.shape[0], BLK), COL) for b in g_blocks]
            + [(b, (b.shape[0], INFO), info_at) for b in g_blocks],
            [((256, width), BF16, (256, BLK), COL), ((256, 64), BF16, (256, 64), FIX)],
            [pltpu.VMEM((256, 64), BF16)],
            2 * 256 * 64 * width,
            2 * 320 * width,
        )
    with jax.named_scope("cot_route"):
        g_rows = lax.all_to_all(g_sent.reshape(16, 16, width), "exp", split_axis=0, concat_axis=0, tiled=True)
        g_rows = g_rows.reshape(256, width)

    with jax.named_scope("tok_pick"):
        *x_sent, x_over, x_mix = call(
            tok_pick_kernel,
            steps,
            [SM(at)]
            + [(b, (32, BLK), lambda i: (0, steps + i)) for b in plane]
            + [(b, (32, INFO), lambda i: (0, 2 * tail)) for b in plane],
            [((32, width), BF16, (32, BLK), COL)] * 4
            + [((128, width), BF16, (128, BLK), COL), ((256, 128), BF16, (256, 128), FIX)],
            [pltpu.VMEM((256, 128), BF16)],
            2 * 256 * 128 * width,
            2 * 400 * width,
            after=[g_mix],
        )
    with jax.named_scope("tok_route"):
        x_rows = [x_sent[0]] + [move_y(x_sent[k], k) for k in (1, 2, 3)]
        x_over = swap_core(x_over)
        x_over = [x_over[k * 32 : k * 32 + 32] for k in range(4)]
        x_rows += [x_over[0]] + [move_y(x_over[k], k) for k in (1, 2, 3)]

    with jax.named_scope("shared"):
        s_hid, s_grads = call(
            shared_kernel,
            steps,
            [(v, (32, BLK), lambda i: (0, steps + i)) for v in plane]
            + [(v, (32, BLK), COL) for v in plane]
            + [(shared_gate.T, (part, BLK), COL), (shared_up.T, (part, BLK), COL), (shared_down, (part, BLK), COL)],
            [((128, part), BF16, (128, part), FIX), ((128, 2 * part), BF16, (128, 2 * part), FIX)],
            [pltpu.VMEM((128, 2 * part), F32), pltpu.VMEM((128, part), F32)],
            6 * 128 * part * width,
            2 * 450 * width,
            after=[x_mix],
        )

    with jax.named_scope("expert"):
        chunks = width // CHUNK
        here = pl.BlockSpec(memory_space=pl.ANY)
        *dx_rows, dx_over, y_rows = pl.pallas_call(
            expert_kernel,
            in_specs=[pl.BlockSpec(memory_space=pltpu.SMEM)] + [here] * 12,
            out_specs=[here] * 6,
            out_shape=[jax.ShapeDtypeStruct((32, width), BF16)] * 4
            + [jax.ShapeDtypeStruct((128, width), BF16), jax.ShapeDtypeStruct((256, width), BF16)],
            scratch_shapes=[
                pltpu.VMEM((256, width), BF16),
                pltpu.VMEM((256, width), BF16),
                pltpu.VMEM((chunks, CHUNK, hidden), BF16),
                pltpu.VMEM((chunks, CHUNK, hidden), BF16),
                pltpu.VMEM((chunks, hidden, CHUNK), BF16),
                pltpu.VMEM((256, width), BF16),
                pltpu.VMEM((256, width), BF16),
                pltpu.SemaphoreType.DMA((14,)),
                pltpu.SemaphoreType.DMA((3, chunks)),
                pltpu.SemaphoreType.DMA((1, chunks)),
            ],
            compiler_params=pltpu.CompilerParams(vmem_limit_bytes=60 * 1024 * 1024),
        )(at, *x_rows, g_rows, expert_gate, expert_up, expert_down)
    with jax.named_scope("out_route"):
        y_home = lax.all_to_all(y_rows.reshape(16, 16, width), "exp", split_axis=0, concat_axis=0, tiled=True)
        y_home = y_home.reshape(256, width)

    with jax.named_scope("back_route"):
        dx_home = [dx_rows[0]] + [move_y(dx_rows[k], -k) for k in (1, 2, 3)]
        dx_over = swap_core(dx_over)
        dx_over = [dx_over[k * 32 : k * 32 + 32] for k in range(4)]
        dx_home += [dx_over[0]] + [move_y(dx_over[k], -k) for k in (1, 2, 3)]
        parts = call(
            back_sum_kernel,
            2 * steps,
            [(v, (32, BLK), later) for v in dx_home]
            + [
                (x_mix, (256, 128), FIX),
                (s_hid, (128, part), FIX),
                (s_grads, (128, 2 * part), FIX),
                (shared_gate.T, (part, BLK), later),
                (shared_up.T, (part, BLK), later),
                (shared_down, (part, BLK), first),
            ],
            [((32, 2 * width), BF16, (32, BLK), COL)] * 4,
            [],
            2 * 256 * 128 * width,
            2 * 400 * width,
            after=[y_home],
        )
        line = ring_sum(move_b, parts).astype(BF16).reshape(4, 8, 2 * width)
        both = ring_sum(move_a, [line[k] for k in range(4)])
        s_out, token_grad = both[:, :width], both[:, width:].astype(BF16)
    with jax.named_scope("out_sum"):
        mine, other = call(
            out_sum_kernel,
            steps,
            [(y_home, (256, BLK), COL), (g_mix, (256, 64), FIX)],
            [((32, width), F32, (32, BLK), COL), ((32, width), BF16, (32, BLK), COL)],
            [],
            2 * 256 * 64 * width,
            2 * 352 * width,
        )
        line = (mine + swap_core(other).astype(F32)).reshape(4, 8, width)
        line = [line[0]] + [line[k].astype(BF16) for k in (1, 2, 3)]
        mixed = (ring_sum(move_y, line) + s_out).astype(BF16)
    return (mixed, token_grad)


def solution(mesh):
    in_specs = (
        P(("grp", "exp"), None),
        P(("grp", "exp"), None),
        P(("grp", "exp"), None),
        P(("grp", "exp"), None),
        P(("grp", "exp"), None, None),
        P(("grp", "exp"), None, None),
        P(("grp", "exp"), None, None),
        P(None, "exp"),
        P(None, "exp"),
        P("exp", None),
    )
    out_specs = (P(("grp", "exp"), None), P(("grp", "exp"), None))
    return jax.shard_map(local, mesh=mesh, in_specs=in_specs, out_specs=out_specs, check_vma=False)
```

```python
import functools

import jax
import jax.numpy as jnp
from jax import lax
from jax.experimental import pallas as pl
from jax.experimental.pallas import tpu as pltpu
from jax.sharding import PartitionSpec as P

SPLIT = 2
TOP = 8
CAP = 2
N_Y, N_X, N_Z = 4, 4, 4
INFO = 128
BLK = 3584
CHUNK = 1792

F32, BF16, I32 = jnp.float32, jnp.bfloat16, jnp.int32


def silu_parts(values):
    logistic = 1.0 / (1.0 + jnp.exp(-values))
    return values * logistic, logistic * (1.0 + values * (1.0 - logistic))


def dot(a, b):
    return jnp.dot(a, b, preferred_element_type=F32)


def dot_t(a, b):
    return lax.dot_general(a, b, (((1,), (1,)), ((), ())), preferred_element_type=F32)


def dot_a(a, b):
    return lax.dot_general(a, b, (((0,), (0,)), ((), ())), preferred_element_type=F32)


def turn(order, v):
    return jnp.dot(order, v, precision=lax.Precision.HIGHEST, preferred_element_type=F32)


def grid_ids(rows, cols):
    return lax.broadcasted_iota(I32, (rows, cols), 0), lax.broadcasted_iota(I32, (rows, cols), 1)


def move_y(v, k):
    return lax.ppermute(v, "grp", [(y * 2 + c, (y + k) % N_Y * 2 + c) for y in range(N_Y) for c in range(2)])


def move_y_apart(v):
    return lax.ppermute(v, "grp", [(y * 2 + c, (y + 1 - 2 * c) % N_Y * 2 + c) for y in range(N_Y) for c in range(2)])


def swap_core(v):
    return lax.ppermute(v, "grp", [(g, g ^ 1) for g in range(N_Y * 2)])


def move_plane(v, k, turned):
    pairs = []
    for grp in range(N_Y * 2):
        for x in range(N_X):
            for z in range(N_Z):
                along_x = (grp % 2 == 0) != turned
                to = (x + k) % N_X * 4 + z if along_x else x * 4 + (z + k) % N_Z
                pairs.append((grp * 16 + x * 4 + z, grp * 16 + to))
    return lax.ppermute(v, ("grp", "exp"), pairs)


def move_a(v, k):
    return move_plane(v, k, False)


def move_b(v, k):
    return move_plane(v, k, True)


def ring(move, v):
    return [v] + [move(v, k) for k in (1, 2, 3)]


def ring_sum(move, parts):
    total = parts[0].astype(F32)
    for k in (1, 2, 3):
        total = total + move(parts[k], -k).astype(F32)
    return total


def call(kernel, grid, ins, outs, scratch, flops, moved, after=()):
    in_specs = [pl.BlockSpec(memory_space=pl.ANY)] * len(after) + [
        pl.BlockSpec(memory_space=pltpu.SMEM) if block == "smem" else pl.BlockSpec(block, at) for _, block, at in ins
    ]
    skip = len(after)
    return pl.pallas_call(
        lambda *refs: kernel(*refs[skip:]),
        grid=(grid,),
        in_specs=in_specs,
        out_specs=[pl.BlockSpec(block, at) for _, _, block, at in outs],
        out_shape=[jax.ShapeDtypeStruct(shape, dtype) for shape, dtype, _, _ in outs],
        scratch_shapes=scratch,
        compiler_params=pltpu.CompilerParams(vmem_limit_bytes=60 * 1024 * 1024),
        cost_estimate=pl.CostEstimate(flops=flops, bytes_accessed=moved, transcendentals=0),
    )(*after, *[a for a, _, _ in ins])


COL = lambda i: (0, i)
FIX = lambda i: (0, 0)


def slots_of(info, expert, block, rank):
    rows = info.shape[0]
    a, b = grid_ids(2 * TOP, INFO)
    across = dot_t((a == b).astype(BF16), info)
    want = expert.astype(F32)
    named = jnp.zeros(expert.shape, F32)
    scale = jnp.zeros(expert.shape, F32)
    for k in range(TOP):
        hit = across[k : k + 1, :] == want
        named = named + jnp.where(hit, 1.0, 0.0)
        scale = scale + jnp.where(hit, across[TOP + k : TOP + k + 1, :], 0.0)
    a, b = grid_ids(rows, rows)
    earlier = jnp.where(((a >> 3) == (b >> 3)) & (a < b), 1.0, 0.0).astype(BF16)
    before = dot(named.astype(BF16), earlier)
    _, row = grid_ids(*expert.shape)
    taken = (named > 0.5) & (before == rank.astype(F32)) & ((row >> 3) == block)
    return jnp.where(taken, 1.0, 0.0).astype(BF16), jnp.where(taken, scale * (1.0 / 256.0), 0.0).astype(BF16)


def cot_pick_kernel(at, g0, g1, g2, i0, i1, i2, sent, mix, hot):
    @pl.when(pl.program_id(0) == 0)
    def _():
        slot, _ = grid_ids(256, 64)
        to, i = grid_ids(64, 64)
        near = 1 + 2 * (at[0] & 1)
        far_near = 4 - near
        came = jnp.zeros((64, 64), I32)
        for n, block in enumerate((0, 4, near, 4 + near, 2, 4 + far_near, far_near, 6)):
            came = jnp.where((i >> 3) == n, block, came)
        order = jnp.where(((to >> 3) == came) & ((to & 7) == (i & 7)), 1.0, 0.0).astype(BF16)
        info = jnp.concatenate([i0[...], i1[...], i2[...]], axis=0)
        one, scaled = slots_of(dot(order, info).astype(BF16), at[0] * 8 + (slot >> 5), (slot >> 1) & 7, slot & 1)
        hot[...] = dot(one, order).astype(BF16)
        mix[...] = scaled

    sent[...] = dot(hot[...], jnp.concatenate([g0[...], g1[...], g2[...]], axis=0)).astype(BF16)


def widen_kernel(tok, cot, routes, weights, all_, g):
    width = tok.shape[1]
    at, to = grid_ids(TOP, INFO)
    place = lambda v, n: dot(v.astype(F32).astype(BF16), jnp.where(to == at + n, 1.0, 0.0).astype(BF16))
    info = (place(routes[...], 0) + place(weights[...], TOP)).astype(BF16)
    all_[:, :width] = cot[...]
    all_[:, width : 2 * width] = tok[...]
    all_[:, 2 * width :] = info
    g[:, :width] = cot[...]
    g[:, width:] = info


def tok_pick_kernel(at, b0, b1, b2, b3, i0, i1, i2, i3, *rest):
    sent, (over, mix, hot) = rest[:4], rest[4:]

    @pl.when(pl.program_id(0) == 0)
    def _():
        slot, _ = grid_ids(256, 128)
        info = jnp.concatenate([i0[...], i1[...], i2[...], i3[...]], axis=0)
        y = (at[0] // 2 + (slot >> 5)) & 3
        c = (at[0] + (slot >> 7)) & 1
        one, scaled = slots_of(info, (y * 2 + c) * 8 + at[1] // SPLIT, (slot >> 1) & 15, slot & 1)
        hot[...] = one
        mix[...] = scaled

    picked = dot(hot[...], jnp.concatenate([b0[...], b1[...], b2[...], b3[...]], axis=0)).astype(BF16)
    for n in range(4):
        sent[n][...] = picked[n * 32 : n * 32 + 32]
    over[...] = picked[128:]


def order_of(at):
    to, i = grid_ids(256, 256)
    from_1 = ((at[0] + (i >> 7)) & 1) == 1
    inner, outer = (i >> 1) & 3, (i >> 3) & 3
    x = (at[1] // 4 - jnp.where(from_1, outer, inner)) & 3
    z = (at[1] - jnp.where(from_1, inner, outer)) & 3
    return jnp.where(to == ((x * 4 + z) * 8 + (i >> 5)) * 2 + (i & 1), 1.0, 0.0)


def expert_kernel(at, _, *refs):
    xs, (g_hbm, gw, uw, dw), dxs, (y_hbm,), (x, g, wg, wu, wd, y, dx, sem, sem_w, sem_o) = (
        refs[:8],
        refs[8:12],
        refs[12:17],
        refs[17:18],
        refs[18:],
    )
    chunks, blk, hidden = wg.shape
    cols = lambda c: pl.ds(pl.multiple_of(c * blk, blk), blk)
    load_x = [pltpu.make_async_copy(v, x.at[pl.ds(n * 32, 32)], sem.at[n]) for n, v in enumerate(xs)]
    load_g = pltpu.make_async_copy(g_hbm, g, sem.at[8])
    load_1 = lambda c: pltpu.make_async_copy(gw.at[0, pl.ds(c * blk, blk)], wg.at[c], sem_w.at[0, c])
    load_2 = lambda c: pltpu.make_async_copy(uw.at[0, pl.ds(c * blk, blk)], wu.at[c], sem_w.at[1, c])
    load_3 = lambda c: pltpu.make_async_copy(dw.at[0, :, cols(c)], wd.at[c], sem_w.at[2, c])
    send_y = lambda c: pltpu.make_async_copy(y.at[:, cols(c)], y_hbm.at[:, cols(c)], sem_o.at[0, c])
    send_dx = [pltpu.make_async_copy(dx.at[pl.ds(n * 32, 32)], v, sem.at[9 + n]) for n, v in enumerate(dxs[:4])]
    send_dx.append(pltpu.make_async_copy(dx.at[pl.ds(128, 128)], dxs[4], sem.at[13]))

    for copy in load_x:
        copy.start()
    for c in range(chunks):
        load_1(c).start()
        load_2(c).start()
    load_g.start()
    for c in range(chunks):
        load_3(c).start()
    for copy in load_x:
        copy.wait()

    def pre(c, accs):
        load_1(c).wait()
        load_2(c).wait()
        rows = x[:, cols(c)]
        return accs[0] + dot(rows, wg[c]), accs[1] + dot(rows, wu[c])

    zero = jnp.zeros((256, hidden), F32)
    gate, up = lax.fori_loop(0, chunks, pre, (zero, zero))
    silu, prime = silu_parts(gate)
    order = order_of(at)
    hid = dot(order.astype(BF16), (silu * up).astype(BF16)).astype(BF16)
    load_g.wait()

    def mid(c, acc):
        load_3(c).wait()
        y[:, cols(c)] = dot(hid, wd[c]).astype(BF16)
        send_y(c).start()
        return acc + dot_t(g[:, cols(c)], wd[c])

    grad = lax.fori_loop(0, chunks, mid, zero)
    grad = lax.dot_general(order, grad, (((0,), (0,)), ((), ())), precision=lax.Precision.HIGHEST, preferred_element_type=F32)
    dg = (grad * (up * prime)).astype(BF16)
    du = (grad * silu).astype(BF16)

    def back(c, _):
        dx[:, cols(c)] = (dot_t(dg, wg[c]) + dot_t(du, wu[c])).astype(BF16)
        return 0

    lax.fori_loop(0, chunks, back, 0)
    for copy in send_dx:
        copy.start()
    for c in range(chunks):
        send_y(c).wait()
    for copy in send_dx:
        copy.wait()


def back_sum_kernel(*refs):
    blocks, (mix, grads, sg, su), outs = refs[:8], refs[8:12], refs[12:]
    rows = jnp.concatenate([v[...] for v in blocks], axis=0)
    total = dot_a(mix[...], rows) + dot(grads[...], jnp.concatenate([sg[...], su[...]], axis=0))
    for n in range(4):
        outs[n][...] = total[n * 32 : n * 32 + 32].astype(BF16)


def shared_out_kernel(hid, sd, *outs):
    total = dot(hid[...], sd[...]).astype(BF16)
    for n in range(4):
        outs[n][...] = total[n * 32 : n * 32 + 32]


def pass_on(v, after):
    here = pl.BlockSpec(memory_space=pl.ANY)
    return pl.pallas_call(
        lambda *refs: None,
        in_specs=[here] * (1 + len(after)),
        out_specs=here,
        out_shape=jax.ShapeDtypeStruct(v.shape, v.dtype),
        input_output_aliases={0: 0},
        compiler_params=pltpu.CompilerParams(vmem_limit_bytes=60 * 1024 * 1024),
    )(v, *after)


def out_sum_kernel(rows, mix, mine, other):
    total = dot_a(mix[...], rows[...])
    mine[...] = total[:32]
    other[...] = total[32:].astype(BF16)


def shared_kernel(*refs):
    xs, gs, (sg, su, sd), (hid, grads, acc, acc_g) = refs[:4], refs[4:8], refs[8:11], refs[11:]
    step = pl.program_id(0)
    part = sg.shape[0]

    @pl.when(step == 0)
    def _():
        acc[...] = jnp.zeros_like(acc)
        acc_g[...] = jnp.zeros_like(acc_g)

    rows = jnp.concatenate([x[...] for x in xs], axis=0)
    acc[...] += dot_t(rows, jnp.concatenate([sg[...], su[...]], axis=0))
    acc_g[...] += dot_t(jnp.concatenate([g[...] for g in gs], axis=0), sd[...])

    @pl.when(step == pl.num_programs(0) - 1)
    def _():
        up = acc[:, part:]
        silu, prime = silu_parts(acc[:, :part])
        hid[...] = (silu * up).astype(BF16)
        grads[:, :part] = (acc_g[...] * up * prime).astype(BF16)
        grads[:, part:] = (acc_g[...] * silu).astype(BF16)


def local(
    tokens,
    routes,
    weights_q,
    cotangent,
    expert_gate,
    expert_up,
    expert_down,
    shared_gate,
    shared_up,
    shared_down,
):
    width = tokens.shape[1]
    hidden = expert_gate.shape[2]
    part = shared_gate.shape[1]
    steps = width // BLK
    tail = width // INFO
    grp, exp = lax.axis_index("grp"), lax.axis_index("exp")
    at = jnp.stack([grp, exp]).astype(I32)
    info = jnp.pad(jnp.concatenate([routes, weights_q], axis=1).astype(BF16), ((0, 0), (0, INFO - 2 * TOP)))
    first = lambda i: (0, jnp.minimum(i, steps - 1))
    later = lambda i: (0, jnp.maximum(i - steps, 0))
    info_at = lambda i: (0, tail)
    SM = lambda a: (a, "smem", None)

    with jax.named_scope("widen"):
        whole = lambda v: (v, v.shape, FIX)
        made = lambda rows, cols: ((rows, cols), BF16, (rows, cols), FIX)
        all_wide, g_wide = call(
            widen_kernel,
            1,
            [whole(v) for v in (tokens, cotangent, routes, weights_q)],
            [made(8, 2 * width + INFO), made(8, width + INFO)],
            [],
            0,
            4 * width * 16,
        )
    with jax.named_scope("gather_line"):
        all_line = ring(move_a, all_wide)
    with jax.named_scope("gather_plane"):
        plane = ring(move_b, jnp.concatenate(all_line, axis=0))
    with jax.named_scope("cot_gather"):
        g_chip = jnp.concatenate([g_wide, swap_core(g_wide)], axis=0)
        g_half = jnp.concatenate([move_y_apart(g_chip), move_y(g_wide, 2)], axis=0)
        g_blocks = [g_chip, g_half, swap_core(g_half)]

    with jax.named_scope("cot_pick"):
        g_sent, g_mix = call(
            cot_pick_kernel,
            steps,
            [SM(at)]
            + [(b, (b.shape[0], BLK), COL) for b in g_blocks]
            + [(b, (b.shape[0], INFO), info_at) for b in g_blocks],
            [((256, width), BF16, (256, BLK), COL), ((256, 64), BF16, (256, 64), FIX)],
            [pltpu.VMEM((256, 64), BF16)],
            2 * 256 * 64 * width,
            2 * 320 * width,
        )
    with jax.named_scope("cot_route"):
        g_rows = lax.all_to_all(g_sent.reshape(16, 16, width), "exp", split_axis=0, concat_axis=0, tiled=True)
        g_rows = g_rows.reshape(256, width)

    with jax.named_scope("tok_pick"):
        *x_sent, x_over, x_mix = call(
            tok_pick_kernel,
            steps,
            [SM(at)]
            + [(b, (32, BLK), lambda i: (0, steps + i)) for b in plane]
            + [(b, (32, INFO), lambda i: (0, 2 * tail)) for b in plane],
            [((32, width), BF16, (32, BLK), COL)] * 4
            + [((128, width), BF16, (128, BLK), COL), ((256, 128), BF16, (256, 128), FIX)],
            [pltpu.VMEM((256, 128), BF16)],
            2 * 256 * 128 * width,
            2 * 400 * width,
            after=[g_mix],
        )
    with jax.named_scope("tok_route"):
        x_rows = [x_sent[0]] + [move_y(x_sent[k], k) for k in (1, 2, 3)]
        x_over = swap_core(x_over)
        x_over = [x_over[k * 32 : k * 32 + 32] for k in range(4)]
        x_rows += [x_over[0]] + [move_y(x_over[k], k) for k in (1, 2, 3)]

    with jax.named_scope("shared"):
        s_hid, s_grads = call(
            shared_kernel,
            steps,
            [(v, (32, BLK), lambda i: (0, steps + i)) for v in plane]
            + [(v, (32, BLK), COL) for v in plane]
            + [(shared_gate.T, (part, BLK), COL), (shared_up.T, (part, BLK), COL), (shared_down, (part, BLK), COL)],
            [((128, part), BF16, (128, part), FIX), ((128, 2 * part), BF16, (128, 2 * part), FIX)],
            [pltpu.VMEM((128, 2 * part), F32), pltpu.VMEM((128, part), F32)],
            6 * 128 * part * width,
            2 * 450 * width,
            after=[x_mix],
        )

    with jax.named_scope("shared_out"):
        s_parts = call(
            shared_out_kernel,
            steps,
            [(s_hid, (128, part), FIX), (shared_down, (part, BLK), COL)],
            [((32, width), BF16, (32, BLK), COL)] * 4,
            [],
            2 * 128 * part * width,
            2 * 192 * width,
            after=x_rows[1:4] + x_rows[5:],
        )
        s_line = ring_sum(move_b, s_parts)

    with jax.named_scope("expert"):
        chunks = width // CHUNK
        here = pl.BlockSpec(memory_space=pl.ANY)
        *dx_rows, dx_over, y_rows = pl.pallas_call(
            expert_kernel,
            in_specs=[pl.BlockSpec(memory_space=pltpu.SMEM)] + [here] * 13,
            out_specs=[here] * 6,
            out_shape=[jax.ShapeDtypeStruct((32, width), BF16)] * 4
            + [jax.ShapeDtypeStruct((128, width), BF16), jax.ShapeDtypeStruct((256, width), BF16)],
            scratch_shapes=[
                pltpu.VMEM((256, width), BF16),
                pltpu.VMEM((256, width), BF16),
                pltpu.VMEM((chunks, CHUNK, hidden), BF16),
                pltpu.VMEM((chunks, CHUNK, hidden), BF16),
                pltpu.VMEM((chunks, hidden, CHUNK), BF16),
                pltpu.VMEM((256, width), BF16),
                pltpu.VMEM((256, width), BF16),
                pltpu.SemaphoreType.DMA((14,)),
                pltpu.SemaphoreType.DMA((3, chunks)),
                pltpu.SemaphoreType.DMA((1, chunks)),
            ],
            compiler_params=pltpu.CompilerParams(vmem_limit_bytes=60 * 1024 * 1024),
        )(at, s_parts[0], *x_rows, g_rows, expert_gate, expert_up, expert_down)
    with jax.named_scope("out_route"):
        y_rows = pass_on(y_rows, [s_line])
        y_home = lax.all_to_all(y_rows.reshape(16, 16, width), "exp", split_axis=0, concat_axis=0, tiled=True)
        y_home = y_home.reshape(256, width)

    with jax.named_scope("back_route"):
        dx_home = [dx_rows[0]] + [move_y(dx_rows[k], -k) for k in (1, 2, 3)]
        dx_over = swap_core(dx_over)
        dx_over = [dx_over[k * 32 : k * 32 + 32] for k in range(4)]
        dx_home += [dx_over[0]] + [move_y(dx_over[k], -k) for k in (1, 2, 3)]
        parts = call(
            back_sum_kernel,
            steps,
            [(v, (32, BLK), COL) for v in dx_home]
            + [
                (x_mix, (256, 128), FIX),
                (s_grads, (128, 2 * part), FIX),
                (shared_gate.T, (part, BLK), COL),
                (shared_up.T, (part, BLK), COL),
            ],
            [((32, width), BF16, (32, BLK), COL)] * 4,
            [],
            2 * 256 * 128 * width,
            2 * 400 * width,
            after=[y_home],
        )
        line = jnp.concatenate([ring_sum(move_b, parts), s_line], axis=1).astype(BF16).reshape(4, 8, 2 * width)
        both = ring_sum(move_a, [line[k] for k in range(4)])
        token_grad, s_out = both[:, :width].astype(BF16), both[:, width:]
    with jax.named_scope("out_sum"):
        mine, other = call(
            out_sum_kernel,
            steps,
            [(y_home, (256, BLK), COL), (g_mix, (256, 64), FIX)],
            [((32, width), F32, (32, BLK), COL), ((32, width), BF16, (32, BLK), COL)],
            [],
            2 * 256 * 64 * width,
            2 * 352 * width,
            after=[parts[0]],
        )
        line = (mine + swap_core(other).astype(F32)).reshape(4, 8, width)
        line = [line[0]] + [line[k].astype(BF16) for k in (1, 2, 3)]
        mixed = (ring_sum(move_y, line) + s_out).astype(BF16)
    return (mixed, token_grad)


def solution(mesh):
    in_specs = (
        P(("grp", "exp"), None),
        P(("grp", "exp"), None),
        P(("grp", "exp"), None),
        P(("grp", "exp"), None),
        P(("grp", "exp"), None, None),
        P(("grp", "exp"), None, None),
        P(("grp", "exp"), None, None),
        P(None, "exp"),
        P(None, "exp"),
        P("exp", None),
    )
    out_specs = (P(("grp", "exp"), None), P(("grp", "exp"), None))
    return jax.shard_map(local, mesh=mesh, in_specs=in_specs, out_specs=out_specs, check_vma=False)
```

```python
import functools

import jax
import jax.numpy as jnp
from jax import lax
from jax.experimental import pallas as pl
from jax.experimental.pallas import tpu as pltpu
from jax.sharding import PartitionSpec as P

SPLIT = 2
TOP = 8
CAP = 2
N_Y, N_X, N_Z = 4, 4, 4
INFO = 128
BLK = 3584
CHUNK = 1792

F32, BF16, I32 = jnp.float32, jnp.bfloat16, jnp.int32


def silu_parts(values):
    logistic = 1.0 / (1.0 + jnp.exp(-values))
    return values * logistic, logistic * (1.0 + values * (1.0 - logistic))


def dot(a, b):
    return jnp.dot(a, b, preferred_element_type=F32)


def dot_t(a, b):
    return lax.dot_general(a, b, (((1,), (1,)), ((), ())), preferred_element_type=F32)


def dot_a(a, b):
    return lax.dot_general(a, b, (((0,), (0,)), ((), ())), preferred_element_type=F32)


def turn(order, v):
    return jnp.dot(order, v, precision=lax.Precision.HIGHEST, preferred_element_type=F32)


def grid_ids(rows, cols):
    return lax.broadcasted_iota(I32, (rows, cols), 0), lax.broadcasted_iota(I32, (rows, cols), 1)


def move_y(v, k):
    return lax.ppermute(v, "grp", [(y * 2 + c, (y + k) % N_Y * 2 + c) for y in range(N_Y) for c in range(2)])


def move_y_apart(v):
    return lax.ppermute(v, "grp", [(y * 2 + c, (y + 1 - 2 * c) % N_Y * 2 + c) for y in range(N_Y) for c in range(2)])


def swap_core(v):
    return lax.ppermute(v, "grp", [(g, g ^ 1) for g in range(N_Y * 2)])


def move_plane(v, k, turned):
    pairs = []
    for grp in range(N_Y * 2):
        for x in range(N_X):
            for z in range(N_Z):
                along_x = (grp % 2 == 0) != turned
                to = (x + k) % N_X * 4 + z if along_x else x * 4 + (z + k) % N_Z
                pairs.append((grp * 16 + x * 4 + z, grp * 16 + to))
    return lax.ppermute(v, ("grp", "exp"), pairs)


def move_a(v, k):
    return move_plane(v, k, False)


def move_b(v, k):
    return move_plane(v, k, True)


def ring(move, v):
    return [v] + [move(v, k) for k in (1, 2, 3)]


def ring_sum(move, parts):
    total = parts[0].astype(F32)
    for k in (1, 2, 3):
        total = total + move(parts[k], -k).astype(F32)
    return total


def call(kernel, grid, ins, outs, scratch, flops, moved, after=()):
    in_specs = [pl.BlockSpec(memory_space=pl.ANY)] * len(after) + [
        pl.BlockSpec(memory_space=pltpu.SMEM) if block == "smem" else pl.BlockSpec(block, at) for _, block, at in ins
    ]
    skip = len(after)
    return pl.pallas_call(
        lambda *refs: kernel(*refs[skip:]),
        grid=(grid,),
        in_specs=in_specs,
        out_specs=[pl.BlockSpec(block, at) for _, _, block, at in outs],
        out_shape=[jax.ShapeDtypeStruct(shape, dtype) for shape, dtype, _, _ in outs],
        scratch_shapes=scratch,
        compiler_params=pltpu.CompilerParams(vmem_limit_bytes=60 * 1024 * 1024),
        cost_estimate=pl.CostEstimate(flops=flops, bytes_accessed=moved, transcendentals=0),
    )(*after, *[a for a, _, _ in ins])


COL = lambda i: (0, i)
FIX = lambda i: (0, 0)


def slots_of(info, expert, block, rank):
    rows = info.shape[0]
    a, b = grid_ids(2 * TOP, INFO)
    across = dot_t((a == b).astype(BF16), info)
    want = expert.astype(F32)
    named = jnp.zeros(expert.shape, F32)
    scale = jnp.zeros(expert.shape, F32)
    for k in range(TOP):
        hit = across[k : k + 1, :] == want
        named = named + jnp.where(hit, 1.0, 0.0)
        scale = scale + jnp.where(hit, across[TOP + k : TOP + k + 1, :], 0.0)
    a, b = grid_ids(rows, rows)
    earlier = jnp.where(((a >> 3) == (b >> 3)) & (a < b), 1.0, 0.0).astype(BF16)
    before = dot(named.astype(BF16), earlier)
    _, row = grid_ids(*expert.shape)
    taken = (named > 0.5) & (before == rank.astype(F32)) & ((row >> 3) == block)
    return jnp.where(taken, 1.0, 0.0).astype(BF16), jnp.where(taken, scale * (1.0 / 256.0), 0.0).astype(BF16)


def cot_pick_kernel(at, g0, g1, g2, i0, i1, i2, sent, mix, hot):
    @pl.when(pl.program_id(0) == 0)
    def _():
        slot, _ = grid_ids(256, 64)
        to, i = grid_ids(64, 64)
        near = 1 + 2 * (at[0] & 1)
        far_near = 4 - near
        came = jnp.zeros((64, 64), I32)
        for n, block in enumerate((0, 4, near, 4 + near, 2, 4 + far_near, far_near, 6)):
            came = jnp.where((i >> 3) == n, block, came)
        order = jnp.where(((to >> 3) == came) & ((to & 7) == (i & 7)), 1.0, 0.0).astype(BF16)
        info = jnp.concatenate([i0[...], i1[...], i2[...]], axis=0)
        one, scaled = slots_of(dot(order, info).astype(BF16), at[0] * 8 + (slot >> 5), (slot >> 1) & 7, slot & 1)
        hot[...] = dot(one, order).astype(BF16)
        mix[...] = scaled

    sent[...] = dot(hot[...], jnp.concatenate([g0[...], g1[...], g2[...]], axis=0)).astype(BF16)


def widen_kernel(tok, cot, routes, weights, all_, g):
    width = tok.shape[1]
    at, to = grid_ids(TOP, INFO)
    place = lambda v, n: dot(v.astype(F32).astype(BF16), jnp.where(to == at + n, 1.0, 0.0).astype(BF16))
    info = (place(routes[...], 0) + place(weights[...], TOP)).astype(BF16)
    all_[:, :width] = cot[...]
    all_[:, width : 2 * width] = tok[...]
    all_[:, 2 * width :] = info
    g[:, :width] = cot[...]
    g[:, width:] = info


def tok_pick_kernel(at, b0, b1, b2, b3, i0, i1, i2, i3, *rest):
    sent, (over, mix, hot) = rest[:4], rest[4:]

    @pl.when(pl.program_id(0) == 0)
    def _():
        slot, _ = grid_ids(256, 128)
        info = jnp.concatenate([i0[...], i1[...], i2[...], i3[...]], axis=0)
        y = (at[0] // 2 + (slot >> 5)) & 3
        c = (at[0] + (slot >> 7)) & 1
        one, scaled = slots_of(info, (y * 2 + c) * 8 + at[1] // SPLIT, (slot >> 1) & 15, slot & 1)
        hot[...] = one
        mix[...] = scaled

    picked = dot(hot[...], jnp.concatenate([b0[...], b1[...], b2[...], b3[...]], axis=0)).astype(BF16)
    for n in range(4):
        sent[n][...] = picked[n * 32 : n * 32 + 32]
    over[...] = picked[128:]


def order_of(at):
    to, i = grid_ids(256, 256)
    from_1 = ((at[0] + (i >> 7)) & 1) == 1
    inner, outer = (i >> 1) & 3, (i >> 3) & 3
    x = (at[1] // 4 - jnp.where(from_1, outer, inner)) & 3
    z = (at[1] - jnp.where(from_1, inner, outer)) & 3
    return jnp.where(to == ((x * 4 + z) * 8 + (i >> 5)) * 2 + (i & 1), 1.0, 0.0)


def expert_kernel(at, _, *refs):
    xs, (g_hbm, gw, uw, dw), dxs, (y_hbm,), (x, g, wg, wu, wd, y, dx, sem, sem_w, sem_o) = (
        refs[:8],
        refs[8:12],
        refs[12:17],
        refs[17:18],
        refs[18:],
    )
    chunks, blk, hidden = wg.shape
    cols = lambda c: pl.ds(pl.multiple_of(c * blk, blk), blk)
    load_x = [pltpu.make_async_copy(v, x.at[pl.ds(n * 32, 32)], sem.at[n]) for n, v in enumerate(xs)]
    load_g = pltpu.make_async_copy(g_hbm, g, sem.at[8])
    load_1 = lambda c: pltpu.make_async_copy(gw.at[0, pl.ds(c * blk, blk)], wg.at[c], sem_w.at[0, c])
    load_2 = lambda c: pltpu.make_async_copy(uw.at[0, pl.ds(c * blk, blk)], wu.at[c], sem_w.at[1, c])
    load_3 = lambda c: pltpu.make_async_copy(dw.at[0, :, cols(c)], wd.at[c], sem_w.at[2, c])
    send_y = lambda c: pltpu.make_async_copy(y.at[:, cols(c)], y_hbm.at[:, cols(c)], sem_o.at[0, c])
    send_dx = [pltpu.make_async_copy(dx.at[pl.ds(n * 32, 32)], v, sem.at[9 + n]) for n, v in enumerate(dxs[:4])]
    send_dx.append(pltpu.make_async_copy(dx.at[pl.ds(128, 128)], dxs[4], sem.at[13]))

    for copy in load_x:
        copy.start()
    for c in range(chunks):
        load_1(c).start()
        load_2(c).start()
    load_g.start()
    for c in range(chunks):
        load_3(c).start()
    for copy in load_x:
        copy.wait()

    def pre(c, accs):
        load_1(c).wait()
        load_2(c).wait()
        rows = x[:, cols(c)]
        return accs[0] + dot(rows, wg[c]), accs[1] + dot(rows, wu[c])

    zero = jnp.zeros((256, hidden), F32)
    gate, up = lax.fori_loop(0, chunks, pre, (zero, zero))
    silu, prime = silu_parts(gate)
    order = order_of(at)
    hid = dot(order.astype(BF16), (silu * up).astype(BF16)).astype(BF16)
    load_g.wait()

    def mid(c, acc):
        load_3(c).wait()
        y[:, cols(c)] = dot(hid, wd[c]).astype(BF16)
        send_y(c).start()
        return acc + dot_t(g[:, cols(c)], wd[c])

    grad = lax.fori_loop(0, chunks, mid, zero)
    grad = lax.dot_general(order, grad, (((0,), (0,)), ((), ())), precision=lax.Precision.HIGHEST, preferred_element_type=F32)
    dg = (grad * (up * prime)).astype(BF16)
    du = (grad * silu).astype(BF16)

    def back(c, _):
        dx[:, cols(c)] = (dot_t(dg, wg[c]) + dot_t(du, wu[c])).astype(BF16)
        return 0

    lax.fori_loop(0, chunks, back, 0)
    for copy in send_dx:
        copy.start()
    for c in range(chunks):
        send_y(c).wait()
    for copy in send_dx:
        copy.wait()


def back_sum_kernel(*refs):
    blocks, (mix, grads, sg, su), outs = refs[:8], refs[8:12], refs[12:]
    rows = jnp.concatenate([v[...] for v in blocks], axis=0)
    total = dot_a(mix[...], rows) + dot(grads[...], jnp.concatenate([sg[...], su[...]], axis=0))
    for n in range(4):
        outs[n][...] = total[n * 32 : n * 32 + 32].astype(BF16)


def shared_out_kernel(hid, sd, l0, l1, l2, l3, mine, line, *both):
    step = pl.program_id(0)
    half = pl.num_programs(0) // 2

    @pl.when(step < half)
    def _():
        total = dot(hid[...], sd[...]).astype(BF16)
        mine[...] = total[:32]
        for n in range(3):
            both[n][...] = total[n * 32 + 32 : n * 32 + 64]

    @pl.when(step >= half)
    def _():
        rows = jnp.concatenate([l0[...], l1[...], l2[...], l3[...]], axis=0)
        line[...] = rows
        for n in range(3):
            both[n][...] = rows


def pass_on(v, after):
    here = pl.BlockSpec(memory_space=pl.ANY)
    return pl.pallas_call(
        lambda *refs: None,
        in_specs=[here] * (1 + len(after)),
        out_specs=here,
        out_shape=jax.ShapeDtypeStruct(v.shape, v.dtype),
        input_output_aliases={0: 0},
        compiler_params=pltpu.CompilerParams(vmem_limit_bytes=60 * 1024 * 1024),
    )(v, *after)


def out_sum_kernel(rows, mix, mine, other):
    total = dot_a(mix[...], rows[...])
    mine[...] = total[:32]
    other[...] = total[32:].astype(BF16)


def shared_kernel(*refs):
    xs, (sg, su, hid, act, slope, acc) = refs[:4], refs[4:]
    step = pl.program_id(0)
    part = sg.shape[0]

    @pl.when(step == 0)
    def _():
        acc[...] = jnp.zeros_like(acc)

    acc[...] += dot_t(jnp.concatenate([x[...] for x in xs], axis=0), jnp.concatenate([sg[...], su[...]], axis=0))

    @pl.when(step == pl.num_programs(0) - 1)
    def _():
        up = acc[:, part:]
        silu, prime = silu_parts(acc[:, :part])
        hid[...] = (silu * up).astype(BF16)
        act[...] = silu
        slope[...] = up * prime


def shared_grad_kernel(*refs):
    gs, (sd, act, slope, grads, acc) = refs[:4], refs[4:]
    step = pl.program_id(0)
    part = sd.shape[0]

    @pl.when(step == 0)
    def _():
        acc[...] = jnp.zeros_like(acc)

    acc[...] += dot_t(jnp.concatenate([g[...] for g in gs], axis=0), sd[...])

    @pl.when(step == pl.num_programs(0) - 1)
    def _():
        grads[:, :part] = (acc[...] * slope[...]).astype(BF16)
        grads[:, part:] = (acc[...] * act[...]).astype(BF16)


def local(
    tokens,
    routes,
    weights_q,
    cotangent,
    expert_gate,
    expert_up,
    expert_down,
    shared_gate,
    shared_up,
    shared_down,
):
    width = tokens.shape[1]
    hidden = expert_gate.shape[2]
    part = shared_gate.shape[1]
    steps = width // BLK
    tail = width // INFO
    grp, exp = lax.axis_index("grp"), lax.axis_index("exp")
    at = jnp.stack([grp, exp]).astype(I32)
    info = jnp.pad(jnp.concatenate([routes, weights_q], axis=1).astype(BF16), ((0, 0), (0, INFO - 2 * TOP)))
    first = lambda i: (0, jnp.minimum(i, steps - 1))
    later = lambda i: (0, jnp.maximum(i - steps, 0))
    info_at = lambda i: (0, tail)
    SM = lambda a: (a, "smem", None)

    with jax.named_scope("widen"):
        whole = lambda v: (v, v.shape, FIX)
        made = lambda rows, cols: ((rows, cols), BF16, (rows, cols), FIX)
        all_wide, g_wide = call(
            widen_kernel,
            1,
            [whole(v) for v in (tokens, cotangent, routes, weights_q)],
            [made(8, 2 * width + INFO), made(8, width + INFO)],
            [],
            0,
            4 * width * 16,
        )
    with jax.named_scope("gather_line"):
        all_line = ring(move_a, all_wide)
    with jax.named_scope("gather_plane"):
        plane = ring(move_b, jnp.concatenate([v[:, width:] for v in all_line], axis=0))
    with jax.named_scope("cot_gather"):
        g_chip = jnp.concatenate([g_wide, swap_core(g_wide)], axis=0)
        g_half = jnp.concatenate([move_y_apart(g_chip), move_y(g_wide, 2)], axis=0)
        g_blocks = [g_chip, g_half, swap_core(g_half)]

    with jax.named_scope("cot_pick"):
        g_sent, g_mix = call(
            cot_pick_kernel,
            steps,
            [SM(at)]
            + [(b, (b.shape[0], BLK), COL) for b in g_blocks]
            + [(b, (b.shape[0], INFO), info_at) for b in g_blocks],
            [((256, width), BF16, (256, BLK), COL), ((256, 64), BF16, (256, 64), FIX)],
            [pltpu.VMEM((256, 64), BF16)],
            2 * 256 * 64 * width,
            2 * 320 * width,
        )
    with jax.named_scope("cot_route"):
        g_rows = lax.all_to_all(g_sent.reshape(16, 16, width), "exp", split_axis=0, concat_axis=0, tiled=True)
        g_rows = g_rows.reshape(256, width)

    with jax.named_scope("tok_pick"):
        *x_sent, x_over, x_mix = call(
            tok_pick_kernel,
            steps,
            [SM(at)]
            + [(b, (32, BLK), COL) for b in plane]
            + [(b, (32, INFO), info_at) for b in plane],
            [((32, width), BF16, (32, BLK), COL)] * 4
            + [((128, width), BF16, (128, BLK), COL), ((256, 128), BF16, (256, 128), FIX)],
            [pltpu.VMEM((256, 128), BF16)],
            2 * 256 * 128 * width,
            2 * 400 * width,
            after=[g_mix],
        )
    with jax.named_scope("tok_route"):
        x_rows = [x_sent[0]] + [move_y(x_sent[k], k) for k in (1, 2, 3)]
        x_over = swap_core(x_over)
        x_over = [x_over[k * 32 : k * 32 + 32] for k in range(4)]
        x_rows += [x_over[0]] + [move_y(x_over[k], k) for k in (1, 2, 3)]

    with jax.named_scope("shared"):
        pre = ((128, part), F32, (128, part), FIX)
        s_hid, s_act, s_slope = call(
            shared_kernel,
            steps,
            [(v, (32, BLK), COL) for v in plane] + [(shared_gate.T, (part, BLK), COL), (shared_up.T, (part, BLK), COL)],
            [((128, part), BF16, (128, part), FIX), pre, pre],
            [pltpu.VMEM((128, 2 * part), F32)],
            4 * 128 * part * width,
            2 * 256 * width,
            after=[x_mix],
        )
    with jax.named_scope("shared_out"):
        s_mine, c_line, *both = call(
            shared_out_kernel,
            2 * steps,
            [(s_hid, (128, part), FIX), (shared_down, (part, BLK), first)] + [(v, (8, BLK), later) for v in all_line],
            [((32, width), BF16, (32, BLK), first), ((32, width), BF16, (32, BLK), later)]
            + [((32, 2 * width), BF16, (32, BLK), COL)] * 3,
            [],
            2 * 128 * part * width,
            2 * 192 * width,
            after=x_rows[1:4] + x_rows[5:],
        )
        both = [move_b(v, -k) for v, k in zip(both, (1, 2, 3), strict=True)]
        s_line = s_mine.astype(F32)
        for v in both:
            s_line = s_line + v[:, :width].astype(F32)

    with jax.named_scope("expert"):
        chunks = width // CHUNK
        here = pl.BlockSpec(memory_space=pl.ANY)
        *dx_rows, dx_over, y_rows = pl.pallas_call(
            expert_kernel,
            in_specs=[pl.BlockSpec(memory_space=pltpu.SMEM)] + [here] * 13,
            out_specs=[here] * 6,
            out_shape=[jax.ShapeDtypeStruct((32, width), BF16)] * 4
            + [jax.ShapeDtypeStruct((128, width), BF16), jax.ShapeDtypeStruct((256, width), BF16)],
            scratch_shapes=[
                pltpu.VMEM((256, width), BF16),
                pltpu.VMEM((256, width), BF16),
                pltpu.VMEM((chunks, CHUNK, hidden), BF16),
                pltpu.VMEM((chunks, CHUNK, hidden), BF16),
                pltpu.VMEM((chunks, hidden, CHUNK), BF16),
                pltpu.VMEM((256, width), BF16),
                pltpu.VMEM((256, width), BF16),
                pltpu.SemaphoreType.DMA((14,)),
                pltpu.SemaphoreType.DMA((3, chunks)),
                pltpu.SemaphoreType.DMA((1, chunks)),
            ],
            compiler_params=pltpu.CompilerParams(vmem_limit_bytes=60 * 1024 * 1024),
        )(at, s_mine, *x_rows, g_rows, expert_gate, expert_up, expert_down)
    with jax.named_scope("out_route"):
        y_rows = pass_on(y_rows, [s_line, *both])
        y_home = lax.all_to_all(y_rows.reshape(16, 16, width), "exp", split_axis=0, concat_axis=0, tiled=True)
        y_home = y_home.reshape(256, width)

    with jax.named_scope("back_route"):
        dx_home = [dx_rows[0]] + [move_y(dx_rows[k], -k) for k in (1, 2, 3)]
        (s_grads,) = call(
            shared_grad_kernel,
            steps,
            [(c_line, (32, BLK), COL)]
            + [(v, (32, BLK), lambda i: (0, steps + i)) for v in reversed(both)]
            + [(shared_down, (part, BLK), COL), (s_act, (128, part), FIX), (s_slope, (128, part), FIX)],
            [((128, 2 * part), BF16, (128, 2 * part), FIX)],
            [pltpu.VMEM((128, part), F32)],
            2 * 128 * part * width,
            2 * 200 * width,
            after=[y_rows],
        )
        dx_over = pass_on(swap_core(dx_over), [s_grads])
        dx_over = [dx_over[k * 32 : k * 32 + 32] for k in range(4)]
        dx_home += [dx_over[0]] + [move_y(dx_over[k], -k) for k in (1, 2, 3)]
        parts = call(
            back_sum_kernel,
            steps,
            [(v, (32, BLK), COL) for v in dx_home]
            + [
                (x_mix, (256, 128), FIX),
                (s_grads, (128, 2 * part), FIX),
                (shared_gate.T, (part, BLK), COL),
                (shared_up.T, (part, BLK), COL),
            ],
            [((32, width), BF16, (32, BLK), COL)] * 4,
            [],
            2 * 256 * 128 * width,
            2 * 400 * width,
            after=[y_home],
        )
        line = jnp.concatenate([ring_sum(move_b, parts), s_line], axis=1).astype(BF16).reshape(4, 8, 2 * width)
        both = ring_sum(move_a, [line[k] for k in range(4)])
        token_grad, s_out = both[:, :width].astype(BF16), both[:, width:]
    with jax.named_scope("out_sum"):
        mine, other = call(
            out_sum_kernel,
            steps,
            [(y_home, (256, BLK), COL), (g_mix, (256, 64), FIX)],
            [((32, width), F32, (32, BLK), COL), ((32, width), BF16, (32, BLK), COL)],
            [],
            2 * 256 * 64 * width,
            2 * 352 * width,
            after=[parts[0]],
        )
        line = (mine + swap_core(other).astype(F32)).reshape(4, 8, width)
        line = [line[0]] + [line[k].astype(BF16) for k in (1, 2, 3)]
        mixed = (ring_sum(move_y, line) + s_out).astype(BF16)
    return (mixed, token_grad)


def solution(mesh):
    in_specs = (
        P(("grp", "exp"), None),
        P(("grp", "exp"), None),
        P(("grp", "exp"), None),
        P(("grp", "exp"), None),
        P(("grp", "exp"), None, None),
        P(("grp", "exp"), None, None),
        P(("grp", "exp"), None, None),
        P(None, "exp"),
        P(None, "exp"),
        P("exp", None),
    )
    out_specs = (P(("grp", "exp"), None), P(("grp", "exp"), None))
    return jax.shard_map(local, mesh=mesh, in_specs=in_specs, out_specs=out_specs, check_vma=False)
```

```python
import functools

import jax
import jax.numpy as jnp
from jax import lax
from jax.experimental import pallas as pl
from jax.experimental.pallas import tpu as pltpu
from jax.sharding import PartitionSpec as P

SPLIT = 2
TOP = 8
CAP = 2
N_Y, N_X, N_Z = 4, 4, 4
INFO = 128
BLK = 3584
CHUNK = 1792

F32, BF16, I32 = jnp.float32, jnp.bfloat16, jnp.int32


def silu_parts(values):
    logistic = 1.0 / (1.0 + jnp.exp(-values))
    return values * logistic, logistic * (1.0 + values * (1.0 - logistic))


def dot(a, b):
    return jnp.dot(a, b, preferred_element_type=F32)


def dot_t(a, b):
    return lax.dot_general(a, b, (((1,), (1,)), ((), ())), preferred_element_type=F32)


def dot_a(a, b):
    return lax.dot_general(a, b, (((0,), (0,)), ((), ())), preferred_element_type=F32)


def turn(order, v):
    return jnp.dot(order, v, precision=lax.Precision.HIGHEST, preferred_element_type=F32)


def grid_ids(rows, cols):
    return lax.broadcasted_iota(I32, (rows, cols), 0), lax.broadcasted_iota(I32, (rows, cols), 1)


def move_y(v, k):
    return lax.ppermute(v, "grp", [(y * 2 + c, (y + k) % N_Y * 2 + c) for y in range(N_Y) for c in range(2)])


def move_y_apart(v):
    return lax.ppermute(v, "grp", [(y * 2 + c, (y + 1 - 2 * c) % N_Y * 2 + c) for y in range(N_Y) for c in range(2)])


def swap_core(v):
    return lax.ppermute(v, "grp", [(g, g ^ 1) for g in range(N_Y * 2)])


def move_plane(v, k, turned):
    pairs = []
    for grp in range(N_Y * 2):
        for x in range(N_X):
            for z in range(N_Z):
                along_x = (grp % 2 == 0) != turned
                to = (x + k) % N_X * 4 + z if along_x else x * 4 + (z + k) % N_Z
                pairs.append((grp * 16 + x * 4 + z, grp * 16 + to))
    return lax.ppermute(v, ("grp", "exp"), pairs)


def move_a(v, k):
    return move_plane(v, k, False)


def move_b(v, k):
    return move_plane(v, k, True)


def ring(move, v):
    return [v] + [move(v, k) for k in (1, 2, 3)]


def ring_sum(move, parts):
    total = parts[0].astype(F32)
    for k in (1, 2, 3):
        total = total + move(parts[k], -k).astype(F32)
    return total


def call(kernel, grid, ins, outs, scratch, flops, moved, after=()):
    in_specs = [pl.BlockSpec(memory_space=pl.ANY)] * len(after) + [
        pl.BlockSpec(memory_space=pltpu.SMEM) if block == "smem" else pl.BlockSpec(block, at) for _, block, at in ins
    ]
    skip = len(after)
    return pl.pallas_call(
        lambda *refs: kernel(*refs[skip:]),
        grid=(grid,),
        in_specs=in_specs,
        out_specs=[pl.BlockSpec(block, at) for _, _, block, at in outs],
        out_shape=[jax.ShapeDtypeStruct(shape, dtype) for shape, dtype, _, _ in outs],
        scratch_shapes=scratch,
        compiler_params=pltpu.CompilerParams(vmem_limit_bytes=60 * 1024 * 1024),
        cost_estimate=pl.CostEstimate(flops=flops, bytes_accessed=moved, transcendentals=0),
    )(*after, *[a for a, _, _ in ins])


COL = lambda i: (0, i)
FIX = lambda i: (0, 0)


def slots_of(info, expert, block, rank):
    rows = info.shape[0]
    a, b = grid_ids(2 * TOP, INFO)
    across = dot_t((a == b).astype(BF16), info)
    want = expert.astype(F32)
    named = jnp.zeros(expert.shape, F32)
    scale = jnp.zeros(expert.shape, F32)
    for k in range(TOP):
        hit = across[k : k + 1, :] == want
        named = named + jnp.where(hit, 1.0, 0.0)
        scale = scale + jnp.where(hit, across[TOP + k : TOP + k + 1, :], 0.0)
    a, b = grid_ids(rows, rows)
    earlier = jnp.where(((a >> 3) == (b >> 3)) & (a < b), 1.0, 0.0).astype(BF16)
    before = dot(named.astype(BF16), earlier)
    _, row = grid_ids(*expert.shape)
    taken = (named > 0.5) & (before == rank.astype(F32)) & ((row >> 3) == block)
    return jnp.where(taken, 1.0, 0.0).astype(BF16), jnp.where(taken, scale * (1.0 / 256.0), 0.0).astype(BF16)


def cot_pick_kernel(at, g0, g1, g2, i0, i1, i2, sent, mix, hot):
    @pl.when(pl.program_id(0) == 0)
    def _():
        slot, _ = grid_ids(256, 64)
        to, i = grid_ids(64, 64)
        near = 1 + 2 * (at[0] & 1)
        far_near = 4 - near
        came = jnp.zeros((64, 64), I32)
        for n, block in enumerate((0, 4, near, 4 + near, 2, 4 + far_near, far_near, 6)):
            came = jnp.where((i >> 3) == n, block, came)
        order = jnp.where(((to >> 3) == came) & ((to & 7) == (i & 7)), 1.0, 0.0).astype(BF16)
        info = jnp.concatenate([i0[...], i1[...], i2[...]], axis=0)
        one, scaled = slots_of(dot(order, info).astype(BF16), at[0] * 8 + (slot >> 5), (slot >> 1) & 7, slot & 1)
        hot[...] = dot(one, order).astype(BF16)
        mix[...] = scaled

    sent[...] = dot(hot[...], jnp.concatenate([g0[...], g1[...], g2[...]], axis=0)).astype(BF16)


def widen_kernel(tok, cot, routes, weights, all_, g):
    width = tok.shape[1]
    at, to = grid_ids(TOP, INFO)
    place = lambda v, n: dot(v.astype(F32).astype(BF16), jnp.where(to == at + n, 1.0, 0.0).astype(BF16))
    info = (place(routes[...], 0) + place(weights[...], TOP)).astype(BF16)
    all_[:, :width] = cot[...]
    all_[:, width : 2 * width] = tok[...]
    all_[:, 2 * width :] = info
    g[:, :width] = cot[...]
    g[:, width:] = info


def tok_pick_kernel(at, b0, b1, b2, b3, i0, i1, i2, i3, *rest):
    sent, (over, mix, hot) = rest[:4], rest[4:]

    @pl.when(pl.program_id(0) == 0)
    def _():
        slot, _ = grid_ids(256, 128)
        info = jnp.concatenate([i0[...], i1[...], i2[...], i3[...]], axis=0)
        y = (at[0] // 2 + (slot >> 5)) & 3
        c = (at[0] + (slot >> 7)) & 1
        one, scaled = slots_of(info, (y * 2 + c) * 8 + at[1] // SPLIT, (slot >> 1) & 15, slot & 1)
        hot[...] = one
        mix[...] = scaled

    picked = dot(hot[...], jnp.concatenate([b0[...], b1[...], b2[...], b3[...]], axis=0)).astype(BF16)
    for n in range(4):
        sent[n][...] = picked[n * 32 : n * 32 + 32]
    over[...] = picked[128:]


def order_of(at):
    to, i = grid_ids(256, 256)
    from_1 = ((at[0] + (i >> 7)) & 1) == 1
    inner, outer = (i >> 1) & 3, (i >> 3) & 3
    x = (at[1] // 4 - jnp.where(from_1, outer, inner)) & 3
    z = (at[1] - jnp.where(from_1, inner, outer)) & 3
    return jnp.where(to == ((x * 4 + z) * 8 + (i >> 5)) * 2 + (i & 1), 1.0, 0.0)


def expert_kernel(at, _, *refs):
    xs, (g_hbm, gw, uw, dw), dxs, (y_hbm,), (x, g, wg, wu, wd, y, dx, sem, sem_w, sem_o) = (
        refs[:8],
        refs[8:12],
        refs[12:17],
        refs[17:18],
        refs[18:],
    )
    chunks, blk, hidden = wg.shape
    cols = lambda c: pl.ds(pl.multiple_of(c * blk, blk), blk)
    load_x = [pltpu.make_async_copy(v, x.at[pl.ds(n * 32, 32)], sem.at[n]) for n, v in enumerate(xs)]
    load_g = pltpu.make_async_copy(g_hbm, g, sem.at[8])
    load_1 = lambda c: pltpu.make_async_copy(gw.at[0, pl.ds(c * blk, blk)], wg.at[c], sem_w.at[0, c])
    load_2 = lambda c: pltpu.make_async_copy(uw.at[0, pl.ds(c * blk, blk)], wu.at[c], sem_w.at[1, c])
    load_3 = lambda c: pltpu.make_async_copy(dw.at[0, :, cols(c)], wd.at[c], sem_w.at[2, c])
    send_y = lambda c: pltpu.make_async_copy(y.at[:, cols(c)], y_hbm.at[:, cols(c)], sem_o.at[0, c])
    send_dx = [pltpu.make_async_copy(dx.at[pl.ds(n * 32, 32)], v, sem.at[9 + n]) for n, v in enumerate(dxs[:4])]
    send_dx.append(pltpu.make_async_copy(dx.at[pl.ds(128, 128)], dxs[4], sem.at[13]))

    for copy in load_x:
        copy.start()
    for c in range(chunks):
        load_1(c).start()
        load_2(c).start()
    load_g.start()
    for c in range(chunks):
        load_3(c).start()
    for copy in load_x:
        copy.wait()

    def pre(c, accs):
        load_1(c).wait()
        load_2(c).wait()
        rows = x[:, cols(c)]
        return accs[0] + dot(rows, wg[c]), accs[1] + dot(rows, wu[c])

    zero = jnp.zeros((256, hidden), F32)
    gate, up = lax.fori_loop(0, chunks, pre, (zero, zero))
    silu, prime = silu_parts(gate)
    order = order_of(at)
    hid = dot(order.astype(BF16), (silu * up).astype(BF16)).astype(BF16)
    load_g.wait()

    def mid(c, acc):
        load_3(c).wait()
        y[:, cols(c)] = dot(hid, wd[c]).astype(BF16)
        send_y(c).start()
        return acc + dot_t(g[:, cols(c)], wd[c])

    grad = lax.fori_loop(0, chunks, mid, zero)
    grad = lax.dot_general(order, grad, (((0,), (0,)), ((), ())), precision=lax.Precision.HIGHEST, preferred_element_type=F32)
    dg = (grad * (up * prime)).astype(BF16)
    du = (grad * silu).astype(BF16)

    def back(c, _):
        dx[:, cols(c)] = (dot_t(dg, wg[c]) + dot_t(du, wu[c])).astype(BF16)
        return 0

    lax.fori_loop(0, chunks, back, 0)
    for copy in send_dx:
        copy.start()
    for c in range(chunks):
        send_y(c).wait()
    for copy in send_dx:
        copy.wait()


def back_sum_kernel(*refs):
    blocks, (mix, grads, sg, su), outs = refs[:8], refs[8:12], refs[12:]
    rows = jnp.concatenate([v[...] for v in blocks], axis=0)
    total = dot_a(mix[...], rows) + dot(grads[...], jnp.concatenate([sg[...], su[...]], axis=0))
    for n in range(4):
        outs[n][...] = total[n * 32 : n * 32 + 32].astype(BF16)


def shared_out_kernel(hid, sd, l0, l1, l2, l3, mine, line, *both):
    step = pl.program_id(0)
    half = pl.num_programs(0) // 2

    @pl.when(step < half)
    def _():
        total = dot(hid[...], sd[...]).astype(BF16)
        mine[...] = total[:32]
        for n in range(3):
            both[n][...] = total[n * 32 + 32 : n * 32 + 64]

    @pl.when(step >= half)
    def _():
        rows = jnp.concatenate([l0[...], l1[...], l2[...], l3[...]], axis=0)
        line[...] = rows
        for n in range(3):
            both[n][...] = rows


def pass_on(v, after):
    here = pl.BlockSpec(memory_space=pl.ANY)
    return pl.pallas_call(
        lambda *refs: None,
        in_specs=[here] * (1 + len(after)),
        out_specs=here,
        out_shape=jax.ShapeDtypeStruct(v.shape, v.dtype),
        input_output_aliases={0: 0},
        compiler_params=pltpu.CompilerParams(vmem_limit_bytes=60 * 1024 * 1024),
    )(v, *after)


def out_sum_kernel(rows, mix, mine, other):
    total = dot_a(mix[...], rows[...])
    mine[...] = total[:32]
    other[...] = total[32:].astype(BF16)


def shared_kernel(*refs):
    xs, (sg, su, hid, act, slope, acc) = refs[:4], refs[4:]
    step = pl.program_id(0)
    part = sg.shape[0]

    @pl.when(step == 0)
    def _():
        acc[...] = jnp.zeros_like(acc)

    acc[...] += dot_t(jnp.concatenate([x[...] for x in xs], axis=0), jnp.concatenate([sg[...], su[...]], axis=0))

    @pl.when(step == pl.num_programs(0) - 1)
    def _():
        up = acc[:, part:]
        silu, prime = silu_parts(acc[:, :part])
        hid[...] = (silu * up).astype(BF16)
        act[...] = silu
        slope[...] = up * prime


def shared_grad_kernel(*refs):
    gs, (sd, act, slope, grads, acc) = refs[:4], refs[4:]
    step = pl.program_id(0)
    part = sd.shape[0]

    @pl.when(step == 0)
    def _():
        acc[...] = jnp.zeros_like(acc)

    acc[...] += dot_t(jnp.concatenate([g[...] for g in gs], axis=0), sd[...])

    @pl.when(step == pl.num_programs(0) - 1)
    def _():
        grads[:, :part] = (acc[...] * slope[...]).astype(BF16)
        grads[:, part:] = (acc[...] * act[...]).astype(BF16)


def local(
    tokens,
    routes,
    weights_q,
    cotangent,
    expert_gate,
    expert_up,
    expert_down,
    shared_gate,
    shared_up,
    shared_down,
):
    width = tokens.shape[1]
    hidden = expert_gate.shape[2]
    part = shared_gate.shape[1]
    steps = width // BLK
    tail = width // INFO
    grp, exp = lax.axis_index("grp"), lax.axis_index("exp")
    at = jnp.stack([grp, exp]).astype(I32)
    info = jnp.pad(jnp.concatenate([routes, weights_q], axis=1).astype(BF16), ((0, 0), (0, INFO - 2 * TOP)))
    first = lambda i: (0, jnp.minimum(i, steps - 1))
    later = lambda i: (0, jnp.maximum(i - steps, 0))
    info_at = lambda i: (0, tail)
    SM = lambda a: (a, "smem", None)

    with jax.named_scope("widen"):
        whole = lambda v: (v, v.shape, FIX)
        made = lambda rows, cols: ((rows, cols), BF16, (rows, cols), FIX)
        all_wide, g_wide = call(
            widen_kernel,
            1,
            [whole(v) for v in (tokens, cotangent, routes, weights_q)],
            [made(8, 2 * width + INFO), made(8, width + INFO)],
            [],
            0,
            4 * width * 16,
        )
    with jax.named_scope("gather_line"):
        all_line = ring(move_a, all_wide)
    with jax.named_scope("gather_plane"):
        plane = ring(move_b, jnp.concatenate([v[:, width:] for v in all_line], axis=0))
    with jax.named_scope("cot_gather"):
        g_chip = jnp.concatenate([g_wide, swap_core(g_wide)], axis=0)
        g_half = jnp.concatenate([move_y_apart(g_chip), move_y(g_wide, 2)], axis=0)
        g_blocks = [g_chip, g_half, swap_core(g_half)]

    with jax.named_scope("cot_pick"):
        g_sent, g_mix = call(
            cot_pick_kernel,
            steps,
            [SM(at)]
            + [(b, (b.shape[0], BLK), COL) for b in g_blocks]
            + [(b, (b.shape[0], INFO), info_at) for b in g_blocks],
            [((256, width), BF16, (256, BLK), COL), ((256, 64), BF16, (256, 64), FIX)],
            [pltpu.VMEM((256, 64), BF16)],
            2 * 256 * 64 * width,
            2 * 320 * width,
        )
    with jax.named_scope("cot_route"):
        g_rows = lax.all_to_all(g_sent.reshape(16, 16, width), "exp", split_axis=0, concat_axis=0, tiled=True)
        g_rows = g_rows.reshape(256, width)

    with jax.named_scope("tok_pick"):
        *x_sent, x_over, x_mix = call(
            tok_pick_kernel,
            steps,
            [SM(at)]
            + [(b, (32, BLK), COL) for b in plane]
            + [(b, (32, INFO), info_at) for b in plane],
            [((32, width), BF16, (32, BLK), COL)] * 4
            + [((128, width), BF16, (128, BLK), COL), ((256, 128), BF16, (256, 128), FIX)],
            [pltpu.VMEM((256, 128), BF16)],
            2 * 256 * 128 * width,
            2 * 400 * width,
            after=[g_mix],
        )
    with jax.named_scope("tok_route"):
        x_rows = [x_sent[0]] + [move_y(x_sent[k], k) for k in (1, 2, 3)]
        x_over = swap_core(x_over)
        x_over = [x_over[k * 32 : k * 32 + 32] for k in range(4)]
        x_rows += [x_over[0]] + [move_y(x_over[k], k) for k in (1, 2, 3)]

    with jax.named_scope("shared"):
        pre = ((128, part), F32, (128, part), FIX)
        s_hid, s_act, s_slope = call(
            shared_kernel,
            steps,
            [(v, (32, BLK), COL) for v in plane] + [(shared_gate.T, (part, BLK), COL), (shared_up.T, (part, BLK), COL)],
            [((128, part), BF16, (128, part), FIX), pre, pre],
            [pltpu.VMEM((128, 2 * part), F32)],
            4 * 128 * part * width,
            2 * 256 * width,
            after=[x_mix],
        )
    with jax.named_scope("shared_out"):
        s_mine, c_line, *both = call(
            shared_out_kernel,
            2 * steps,
            [(s_hid, (128, part), FIX), (shared_down, (part, BLK), first)] + [(v, (8, BLK), later) for v in all_line],
            [((32, width), BF16, (32, BLK), first), ((32, width), BF16, (32, BLK), later)]
            + [((32, 2 * width), BF16, (32, BLK), COL)] * 3,
            [],
            2 * 128 * part * width,
            2 * 192 * width,
            after=x_rows[1:4] + x_rows[5:],
        )
        both = [move_b(v, -k) for v, k in zip(both, (1, 2, 3), strict=True)]
        s_line = s_mine.astype(F32)
        for v in both:
            s_line = s_line + v[:, :width].astype(F32)

    with jax.named_scope("expert"):
        chunks = width // CHUNK
        here = pl.BlockSpec(memory_space=pl.ANY)
        *dx_rows, dx_over, y_rows = pl.pallas_call(
            expert_kernel,
            in_specs=[pl.BlockSpec(memory_space=pltpu.SMEM)] + [here] * 13,
            out_specs=[here] * 6,
            out_shape=[jax.ShapeDtypeStruct((32, width), BF16)] * 4
            + [jax.ShapeDtypeStruct((128, width), BF16), jax.ShapeDtypeStruct((256, width), BF16)],
            scratch_shapes=[
                pltpu.VMEM((256, width), BF16),
                pltpu.VMEM((256, width), BF16),
                pltpu.VMEM((chunks, CHUNK, hidden), BF16),
                pltpu.VMEM((chunks, CHUNK, hidden), BF16),
                pltpu.VMEM((chunks, hidden, CHUNK), BF16),
                pltpu.VMEM((256, width), BF16),
                pltpu.VMEM((256, width), BF16),
                pltpu.SemaphoreType.DMA((14,)),
                pltpu.SemaphoreType.DMA((3, chunks)),
                pltpu.SemaphoreType.DMA((1, chunks)),
            ],
            compiler_params=pltpu.CompilerParams(vmem_limit_bytes=60 * 1024 * 1024),
        )(at, s_mine, *x_rows, g_rows, expert_gate, expert_up, expert_down)
    with jax.named_scope("out_route"):
        y_rows = pass_on(y_rows, [s_line, *both])
        y_home = lax.all_to_all(y_rows.reshape(16, 16, width), "exp", split_axis=0, concat_axis=0, tiled=True)
        y_home = y_home.reshape(256, width)

    with jax.named_scope("back_route"):
        dx_home = [dx_rows[0]] + [move_y(dx_rows[k], -k) for k in (1, 2, 3)]
        (s_grads,) = call(
            shared_grad_kernel,
            steps,
            [(c_line, (32, BLK), COL)]
            + [(v, (32, BLK), lambda i: (0, steps + i)) for v in reversed(both)]
            + [(shared_down, (part, BLK), COL), (s_act, (128, part), FIX), (s_slope, (128, part), FIX)],
            [((128, 2 * part), BF16, (128, 2 * part), FIX)],
            [pltpu.VMEM((128, part), F32)],
            2 * 128 * part * width,
            2 * 200 * width,
            after=[y_rows],
        )
        dx_over = pass_on(swap_core(dx_over), [s_grads])
        dx_over = [dx_over[k * 32 : k * 32 + 32] for k in range(4)]
        dx_home += [dx_over[0]] + [move_y(dx_over[k], -k) for k in (1, 2, 3)]
        parts = call(
            back_sum_kernel,
            steps,
            [(v, (32, BLK), COL) for v in dx_home]
            + [
                (x_mix, (256, 128), FIX),
                (s_grads, (128, 2 * part), FIX),
                (shared_gate.T, (part, BLK), COL),
                (shared_up.T, (part, BLK), COL),
            ],
            [((32, width), BF16, (32, BLK), COL)] * 4,
            [],
            2 * 256 * 128 * width,
            2 * 400 * width,
            after=[y_home],
        )
    with jax.named_scope("out_sum"):
        mine, other = call(
            out_sum_kernel,
            steps,
            [(y_home, (256, BLK), COL), (g_mix, (256, 64), FIX)],
            [((32, width), F32, (32, BLK), COL), ((32, width), BF16, (32, BLK), COL)],
            [],
            2 * 256 * 64 * width,
            2 * 352 * width,
            after=[parts[0]],
        )
        line = (mine + swap_core(other).astype(F32)).reshape(4, 8, width)
        home = [move_y(line[k].astype(BF16), -k) for k in (1, 2, 3)]
        s_line = pass_on(s_line, home)
    with jax.named_scope("back_sum"):
        y_sum = line[0]
        for v in home:
            y_sum = y_sum + v.astype(F32)
        line = jnp.concatenate([ring_sum(move_b, parts), s_line], axis=1).astype(BF16).reshape(4, 8, 2 * width)
        both = ring_sum(move_a, [line[k] for k in range(4)])
        token_grad, s_out = both[:, :width].astype(BF16), both[:, width:]
        mixed = (y_sum + s_out).astype(BF16)
    return (mixed, token_grad)


def solution(mesh):
    in_specs = (
        P(("grp", "exp"), None),
        P(("grp", "exp"), None),
        P(("grp", "exp"), None),
        P(("grp", "exp"), None),
        P(("grp", "exp"), None, None),
        P(("grp", "exp"), None, None),
        P(("grp", "exp"), None, None),
        P(None, "exp"),
        P(None, "exp"),
        P("exp", None),
    )
    out_specs = (P(("grp", "exp"), None), P(("grp", "exp"), None))
    return jax.shard_map(local, mesh=mesh, in_specs=in_specs, out_specs=out_specs, check_vma=False)
```
